32 devices in a mesh: chan: 4 (over z), sx: 4 (over x, core), sy: 2 (over y).
Axes of the slice: x: 2, y: 2, z: 4, core: 2. Of those that a mesh axis runs over, the one named last changes fastest.
Arguments:
- volume: bfloat16 [4, 16, 64, 256], P('sx', 'sy', None, 'chan'), may hold values from -6 to 6
- kernel: bfloat16 [27, 256, 256], P(None, 'chan'), may hold values from -0.078125 to 0.078125
- grad_out: bfloat16 [4, 16, 64, 256], P('sx', 'sy', None, 'chan'), may hold values from -6 to 6
Outputs:
- out: bfloat16 [4, 16, 64, 256], P('sx', 'sy', None, 'chan')
- grad_input: bfloat16 [4, 16, 64, 256], P('sx', 'sy', None, 'chan')
- grad_kernel: float32 [27, 256, 256], P(None, 'chan')
The draws below stay inside these ranges and needn't reach their ends.
All inputs are finite; a program needn't handle non-finite values.
Results may differ from the reference program's by a relative error of at most 0.0015.
Values may be sent and summed in bfloat16 or wider, within the bound.
A program may use at most 64 MiB of HBM per device.

```python
import math
import jax
import jax.numpy as jnp

CIN = 256
COUT = 256
NX = 4
NY = 16
NZ = 64


def block_levels(stream_key, shape, cuts, least, largest):
    loudness = 1.0
    for axis_at, blocks in cuts:
        heights = jax.random.uniform(jax.random.fold_in(jax.random.fold_in(stream_key, 6), axis_at), (blocks,), jnp.float32, least / len(cuts), largest / len(cuts))
        loudness = loudness * jnp.repeat(jnp.exp(heights), shape[axis_at] // blocks).reshape((-1,) + (1,) * (len(shape) - 1 - axis_at))
    return loudness


def bell_draw(rng, dims, width, limit, shards=(), dtype=jnp.bfloat16):
    loudness = block_levels(rng, dims, shards, -0.22, 0.18) if shards else 1.0
    values = jax.random.normal(rng, dims, jnp.float32) * width * loudness
    return jnp.minimum(jnp.maximum(values, -limit), limit).astype(dtype)


def setup_inputs(seed: int = 0) -> dict:
    key_of = jax.random.split(jax.random.key(seed), 4)
    return {
        "volume": bell_draw(key_of[0], (NX, NY, NZ, CIN), 1.0, 6.0, ((0, 4), (1, 2), (3, 4))),
        "kernel": bell_draw(key_of[1], (27, CIN, COUT), (27 * CIN) ** -0.5, 0.078125, ((1, 4),)),
        "grad_out": bell_draw(key_of[2], (NX, NY, NZ, COUT), 1.0, 6.0, ((0, 4), (1, 2), (3, 4))),
    }


def reference(volume, kernel, grad_out):
    padded = jnp.pad(volume, ((1, 1), (1, 1), (1, 1), (0, 0)))
    grad_pad = jnp.pad(grad_out, ((1, 1), (1, 1), (1, 1), (0, 0)))
    flat_grad = grad_out.reshape(-1, COUT)
    result = jnp.zeros((NX * NY * NZ, COUT), jnp.float32)
    back = jnp.zeros((NX * NY * NZ, CIN), jnp.float32)
    kernel_terms = []
    for index in range(27):
        first, second, third = (index // 9, index // 3 % 3, index % 3)
        window = padded[first:first + NX, second:second + NY, third:third + NZ].reshape(-1, CIN)
        result = result + jnp.dot(window, kernel[index], preferred_element_type=jnp.float32)
        grad_win = grad_pad[2 - first:2 - first + NX, 2 - second:2 - second + NY, 2 - third:2 - third + NZ].reshape(-1, COUT)
        back = back + jnp.dot(grad_win, kernel[index].T, preferred_element_type=jnp.float32)
        kernel_terms.append(jnp.dot(window.T, flat_grad, preferred_element_type=jnp.float32))
    out = result.reshape(NX, NY, NZ, COUT).astype(jnp.bfloat16)
    grad_input = back.reshape(NX, NY, NZ, CIN).astype(jnp.bfloat16)
    grad_kernel = jnp.stack(kernel_terms) / jnp.float32(math.sqrt(NX * NY * NZ))
    return (out, grad_input, grad_kernel)
```

```python
import functools
import math

import jax
import jax.numpy as jnp
from jax import lax
from jax.experimental import pallas as pl
from jax.experimental.pallas import tpu as pltpu
from jax.sharding import PartitionSpec as P


def padded_2(shard, sides, width):
    for axis, dim in sides:
        count, length = (lax.axis_size(axis), shard.shape[dim])
        up = [(i, (i + 1) % count) for i in range(count - 1)]
        down = [(j, i) for i, j in up]
        last = lax.slice_in_dim(shard, length - width, length, axis=dim)
        leading = lax.slice_in_dim(shard, 0, width, axis=dim)
        before = lax.ppermute(last, axis, up)
        after = lax.ppermute(leading, axis, down)
        shard = jnp.concatenate([before, shard, after], axis=dim)
    return shard


def body(volume, kernel, grad_out):
    size_x, size_y, size_z, own_in = volume.shape
    total_out = kernel.shape[2]
    cells = size_x * size_y * size_z
    rim = padded_2(volume, (("sx", 0), ("sy", 1)), 1)
    padded = jnp.pad(rim, ((0, 0), (0, 0), (1, 1), (0, 0)))
    offsets = [(index // 9, index // 3 % 3, index % 3) for index in range(27)]
    partial_out = jnp.zeros((cells, total_out), jnp.float32)
    for index in range(27):
        a, b, e = offsets[index]
        window = padded[a : a + size_x, b : b + size_y, e : e + size_z].reshape(cells, own_in)
        partial_out = partial_out + jnp.dot(
            window, kernel[index], preferred_element_type=jnp.float32
        )
    partial_out = partial_out.reshape(size_x, size_y, size_z, total_out)
    out = lax.psum_scatter(partial_out, "chan", scatter_dimension=3, tiled=True).astype(
        jnp.bfloat16
    )
    grad_full = lax.all_gather(grad_out, "chan", axis=3, tiled=True)
    grad_rimmed = padded_2(grad_full, (("sx", 0), ("sy", 1)), 1)
    grad_padded = jnp.pad(grad_rimmed, ((0, 0), (0, 0), (1, 1), (0, 0)))
    flat_grad = grad_full.reshape(cells, total_out)
    back = jnp.zeros((cells, own_in), jnp.float32)
    kernel_terms = []
    for index in range(27):
        a, b, e = offsets[index]
        window = grad_padded[
            2 - a : 2 - a + size_x, 2 - b : 2 - b + size_y, 2 - e : 2 - e + size_z
        ].reshape(cells, total_out)
        back = back + lax.dot_general(
            window, kernel[index], (((1,), (1,)), ((), ())), preferred_element_type=jnp.float32
        )
        in_window = padded[a : a + size_x, b : b + size_y, e : e + size_z].reshape(cells, own_in)
        kernel_terms.append(
            lax.dot_general(
                in_window, flat_grad, (((0,), (0,)), ((), ())), preferred_element_type=jnp.float32
            )
        )
    grad_input = back.reshape(size_x, size_y, size_z, own_in).astype(jnp.bfloat16)
    local_kernel = jnp.stack(kernel_terms)
    summed = lax.psum(local_kernel, ("sx", "sy"))
    all_cells = cells * lax.axis_size("sx") * lax.axis_size("sy")
    grad_kernel = summed / jnp.float32(math.sqrt(all_cells))
    return (out, grad_input, grad_kernel)


MESH = pl.DeviceIdType.MESH
F32 = jnp.float32
BF16 = jnp.bfloat16


def fused_kernel(
    vol_ref, w_ref, g_ref, out_ref, gi_ref, gk_ref,
    blocks, gpad, v3, vt, part, got, z_send, z_recv, p_send, p_recv, r_send, r_recv,
    *, scale,
):
    chans, count_s, count_h = lax.axis_size("chan"), lax.axis_size("sx"), lax.axis_size("sy")
    c, s, h = lax.axis_index("chan"), lax.axis_index("sx"), lax.axis_index("sy")
    rows_y, size_z, ch = vol_ref.shape[1:]
    half = rows_y // 2
    cells = half * size_z
    total = w_ref.shape[2]
    wide = 3 * ch
    core, far_s, far_h = s + 1 - 2 * (s % 2), (s + 2) % 4, 1 - h
    others = (c + 1 - 2 * (c % 2), (c + 2) % 4, 3 - c)
    to_x, to_y, to_core = {"sx": far_s}, {"sy": far_h}, {"sx": core}
    sent = []

    def remote(src, dst, send, recv, where):
        return pltpu.make_async_remote_copy(
            src_ref=src, dst_ref=dst, send_sem=send, recv_sem=recv,
            device_id=where, device_id_type=MESH,
        )

    def push(src, send, recv, where, dst=None):
        copy = remote(src, src if dst is None else dst, send, recv, where)
        copy.start()
        sent.append(copy)

    def arrived(ref, send, recv, where):
        remote(ref, ref, send, recv, where).wait_recv()

    for index, ref in ((c, g_ref), (chans, vol_ref)):
        blocks[index, s, h, :, :, :ch] = ref[0, :half]
        blocks[index, s, h, :, :, ch:] = ref[0, half:]

    barrier = pltpu.get_barrier_semaphore()
    partners = [{"chan": d} for d in others] + [to_x, to_y, to_core]
    for where in partners:
        pl.semaphore_signal(barrier, inc=1, device_id=where, device_id_type=MESH)
    pl.semaphore_wait(barrier, len(partners))

    def offer(k, index):
        own = blocks.at[index, s, h]
        push(own, p_send.at[k, 0], p_recv.at[k, 0], to_x)
        push(own, p_send.at[k, 1], p_recv.at[k, 1], to_y)
        push(own, p_send.at[k, 2], p_recv.at[k, 2], to_core)

    def relay(k, index):
        from_x, from_y = blocks.at[index, far_s, h], blocks.at[index, s, far_h]
        cut = half // 2
        arrived(from_x, p_send.at[k, 0], p_recv.at[k, 0], to_x)
        push(from_x.at[:cut], p_send.at[k, 3], p_recv.at[k, 3], to_y)
        push(from_x, p_send.at[k, 5], p_recv.at[k, 5], to_core)
        arrived(from_y, p_send.at[k, 1], p_recv.at[k, 1], to_y)
        push(from_y.at[cut:], p_send.at[k, 4], p_recv.at[k, 4], to_x)
        push(from_y, p_send.at[k, 6], p_recv.at[k, 6], to_core)

    def corner(k, index):
        diag = blocks.at[index, far_s, far_h]
        cut = half // 2
        arrived(diag.at[:cut], p_send.at[k, 3], p_recv.at[k, 3], to_y)
        arrived(diag.at[cut:], p_send.at[k, 4], p_recv.at[k, 4], to_x)
        push(diag, p_send.at[k, 7], p_recv.at[k, 7], to_core)

    def from_core(k, index):
        far_core = 3 - s
        arrived(blocks.at[index, core, h], p_send.at[k, 2], p_recv.at[k, 2], to_core)
        arrived(blocks.at[index, far_core, h], p_send.at[k, 5], p_recv.at[k, 5], to_core)
        arrived(blocks.at[index, core, far_h], p_send.at[k, 6], p_recv.at[k, 6], to_core)
        arrived(blocks.at[index, far_core, far_h], p_send.at[k, 7], p_recv.at[k, 7], to_core)

    def from_chan(j):
        index = others[j]
        arrived(blocks.at[index, s, h], z_send.at[j], z_recv.at[j], {"chan": index})
        offer(j + 2, index)

    offer(0, chans)
    for j, d in enumerate(others):
        push(blocks.at[c, s, h], z_send.at[j], z_recv.at[j], {"chan": d})
    offer(1, c)

    zero_row = jnp.zeros((size_z, total), BF16)
    zero_v = jnp.zeros((size_z, wide), BF16)
    last_x, last_y = gpad.shape[0] - 1, gpad.shape[1] - 1

    @pl.loop(0, gpad.shape[1])
    def _(y):
        for x in (0, last_x):
            gpad[x, y] = zero_row
            v3[x, y] = zero_v

    for x in range(1, last_x):
        for y in (0, last_y):
            gpad[x, y] = zero_row
            v3[x, y] = zero_v

    relay(0, chans)
    corner(0, chans)
    from_chan(0)
    relay(1, c)
    from_core(0, chans)

    row = lax.broadcasted_iota(jnp.int32, (cells, 2 * ch), 0) % size_z

    def spread(x, hy):
        centre = blocks[chans, x, hy].reshape(cells, 2 * ch)
        wide_centre = centre.astype(F32)
        before = jnp.where(row == 0, 0.0, pltpu.roll(wide_centre, 1, 0))
        after = jnp.where(row == size_z - 1, 0.0, pltpu.roll(wide_centre, cells - 1, 0))
        for e, moved in enumerate((before, wide_centre, after)):
            narrow = moved.astype(BF16).reshape(half, size_z, 2 * ch)
            turned = moved.T.astype(BF16)
            for k in range(2):
                v3[x + 1, pl.ds(1 + hy * rows_y + k * half, half), :, e * ch : (e + 1) * ch] = (
                    narrow[:, :, k * ch : (k + 1) * ch]
                )
                vt[x, hy * 2 + k, e * ch : (e + 1) * ch, :] = turned[k * ch : (k + 1) * ch]

    @pl.loop(0, count_s * count_h)
    def _(n):
        spread(n // count_h, n % count_h)

    corner(1, c)
    relay(2, others[0])
    from_chan(1)

    @pl.loop(0, 2)
    def _(t):
        acc = jnp.zeros((cells, total), F32)
        for a in range(3):
            for b in range(3):
                window = v3[s + a, pl.ds(h * rows_y + t * half + b, half)].reshape(cells, wide)
                acc = acc + jnp.dot(window, w_ref[3 * a + b], preferred_element_type=F32)
        part[t] = acc

    for d in range(chans):
        for k in range(2):
            got[chans + d, :, k * ch : (k + 1) * ch] = part[k, :, d * ch : (d + 1) * ch]

    for j, d in enumerate(others):
        push(got.at[chans + d], r_send.at[j], r_recv.at[j], {"chan": d}, dst=got.at[c])

    corner(2, others[0])
    relay(3, others[1])
    from_chan(2)
    corner(3, others[1])
    relay(4, others[2])
    corner(4, others[2])
    for k, index in enumerate((c,) + others):
        from_core(k + 1, index)

    @pl.loop(0, count_s * count_h)
    def _(n):
        x, hy = n // count_h, n % count_h
        for d in range(chans):
            for k in range(2):
                gpad[x + 1, pl.ds(1 + hy * rows_y + k * half, half), :, d * ch : (d + 1) * ch] = (
                    blocks[d, x, hy, :, :, k * ch : (k + 1) * ch]
                )

    row_out = lax.broadcasted_iota(jnp.int32, (cells, ch), 0) % size_z

    @pl.loop(0, 2)
    def _(t):
        acc = jnp.zeros((cells, wide), F32)
        for a in range(3):
            for b in range(3):
                window = gpad[s + 2 - a, pl.ds(h * rows_y + t * half + 2 - b, half)]
                acc = acc + lax.dot_general(
                    window.reshape(cells, total), w_ref[3 * a + b],
                    (((1,), (1,)), ((), ())), preferred_element_type=F32,
                )
        first, middle, final = acc[:, :ch], acc[:, ch : 2 * ch], acc[:, 2 * ch :]
        later = jnp.where(row_out == size_z - 1, 0.0, pltpu.roll(first, cells - 1, 0))
        sooner = jnp.where(row_out == 0, 0.0, pltpu.roll(final, 1, 0))
        gi_ref[0, pl.ds(t * half, half)] = (
            (later + middle + sooner).astype(BF16).reshape(half, size_z, ch)
        )

    for a in range(3):

        @pl.loop(0, 3)
        def _(b):
            acc = jnp.zeros((wide, total), F32)
            for x in range(count_s):
                if 0 <= x + 1 - a < count_s:
                    for t in range(2 * count_h):
                        rows = gpad[x + 2 - a, pl.ds(2 - b + t * half, half)]
                        acc = acc + jnp.dot(
                            vt[x, t], rows.reshape(cells, total), preferred_element_type=F32
                        )
            gk_ref[3 * a + b] = acc / scale

    for j, d in enumerate(others):
        arrived(got.at[d], r_send.at[j], r_recv.at[j], {"chan": d})
    summed = got[chans + c]
    for d in others:
        summed = summed + got[d]
    narrow = summed.astype(BF16).reshape(half, size_z, 2 * ch)
    out_ref[0, :half] = narrow[:, :, :ch]
    out_ref[0, half:] = narrow[:, :, ch:]
    for copy in sent:
        copy.wait_send()


def fused_body(volume, kernel, grad_out):
    chans, count_s, count_h = lax.axis_size("chan"), lax.axis_size("sx"), lax.axis_size("sy")
    _, rows_y, size_z, ch = volume.shape
    total = kernel.shape[2]
    half, wide = rows_y // 2, 3 * ch
    cells = half * size_z
    all_y = rows_y * count_h
    scale = math.sqrt(count_s * all_y * size_z)
    weights = kernel.reshape(9, wide, total)
    vmem = pl.BlockSpec(memory_space=pltpu.VMEM)
    dma = pltpu.SemaphoreType.DMA
    out, gi, gk = pl.pallas_call(
        functools.partial(fused_kernel, scale=scale),
        out_shape=(
            jax.ShapeDtypeStruct(volume.shape, BF16),
            jax.ShapeDtypeStruct(volume.shape, BF16),
            jax.ShapeDtypeStruct(weights.shape, F32),
        ),
        in_specs=[vmem] * 3,
        out_specs=(vmem,) * 3,
        scratch_shapes=[
            pltpu.VMEM((chans + 1, count_s, count_h, half, size_z, 2 * ch), BF16),
            pltpu.VMEM((count_s + 2, all_y + 2, size_z, total), BF16),
            pltpu.VMEM((count_s + 2, all_y + 2, size_z, wide), BF16),
            pltpu.VMEM((count_s, 2 * count_h, wide, cells), BF16),
            pltpu.VMEM((2, cells, total), F32),
            pltpu.VMEM((2 * chans, cells, 2 * ch), F32),
            dma((chans - 1,)), dma((chans - 1,)),
            dma((chans + 1, 8)), dma((chans + 1, 8)),
            dma((chans - 1,)), dma((chans - 1,)),
        ],
        compiler_params=pltpu.CompilerParams(
            collective_id=0, has_side_effects=True, vmem_limit_bytes=50 * 2**20
        ),
    )(volume, weights, grad_out)
    return out, gi, gk.reshape(kernel.shape)


def solution(mesh):
    small = (mesh.shape["chan"], mesh.shape["sx"], mesh.shape["sy"]) == (4, 4, 2)
    return jax.shard_map(
        fused_body if small else body,
        mesh=mesh,
        in_specs=(P("sx", "sy", None, "chan"), P(None, "chan", None), P("sx", "sy", None, "chan")),
        out_specs=(P("sx", "sy", None, "chan"), P("sx", "sy", None, "chan"), P(None, "chan", None)),
        check_vma=False,
    )
```

```python
import functools
import math

import jax
import jax.numpy as jnp
from jax import lax
from jax.experimental import pallas as pl
from jax.experimental.pallas import tpu as pltpu
from jax.sharding import PartitionSpec as P


def padded_2(shard, sides, width):
    for axis, dim in sides:
        count, length = (lax.axis_size(axis), shard.shape[dim])
        up = [(i, (i + 1) % count) for i in range(count - 1)]
        down = [(j, i) for i, j in up]
        last = lax.slice_in_dim(shard, length - width, length, axis=dim)
        leading = lax.slice_in_dim(shard, 0, width, axis=dim)
        before = lax.ppermute(last, axis, up)
        after = lax.ppermute(leading, axis, down)
        shard = jnp.concatenate([before, shard, after], axis=dim)
    return shard


def body(volume, kernel, grad_out):
    size_x, size_y, size_z, own_in = volume.shape
    total_out = kernel.shape[2]
    cells = size_x * size_y * size_z
    rim = padded_2(volume, (("sx", 0), ("sy", 1)), 1)
    padded = jnp.pad(rim, ((0, 0), (0, 0), (1, 1), (0, 0)))
    offsets = [(index // 9, index // 3 % 3, index % 3) for index in range(27)]
    partial_out = jnp.zeros((cells, total_out), jnp.float32)
    for index in range(27):
        a, b, e = offsets[index]
        window = padded[a : a + size_x, b : b + size_y, e : e + size_z].reshape(cells, own_in)
        partial_out = partial_out + jnp.dot(
            window, kernel[index], preferred_element_type=jnp.float32
        )
    partial_out = partial_out.reshape(size_x, size_y, size_z, total_out)
    out = lax.psum_scatter(partial_out, "chan", scatter_dimension=3, tiled=True).astype(
        jnp.bfloat16
    )
    grad_full = lax.all_gather(grad_out, "chan", axis=3, tiled=True)
    grad_rimmed = padded_2(grad_full, (("sx", 0), ("sy", 1)), 1)
    grad_padded = jnp.pad(grad_rimmed, ((0, 0), (0, 0), (1, 1), (0, 0)))
    flat_grad = grad_full.reshape(cells, total_out)
    back = jnp.zeros((cells, own_in), jnp.float32)
    kernel_terms = []
    for index in range(27):
        a, b, e = offsets[index]
        window = grad_padded[
            2 - a : 2 - a + size_x, 2 - b : 2 - b + size_y, 2 - e : 2 - e + size_z
        ].reshape(cells, total_out)
        back = back + lax.dot_general(
            window, kernel[index], (((1,), (1,)), ((), ())), preferred_element_type=jnp.float32
        )
        in_window = padded[a : a + size_x, b : b + size_y, e : e + size_z].reshape(cells, own_in)
        kernel_terms.append(
            lax.dot_general(
                in_window, flat_grad, (((0,), (0,)), ((), ())), preferred_element_type=jnp.float32
            )
        )
    grad_input = back.reshape(size_x, size_y, size_z, own_in).astype(jnp.bfloat16)
    local_kernel = jnp.stack(kernel_terms)
    summed = lax.psum(local_kernel, ("sx", "sy"))
    all_cells = cells * lax.axis_size("sx") * lax.axis_size("sy")
    grad_kernel = summed / jnp.float32(math.sqrt(all_cells))
    return (out, grad_input, grad_kernel)


MESH = pl.DeviceIdType.MESH
F32 = jnp.float32
BF16 = jnp.bfloat16


def fused_kernel(
    vol_hbm, w_hbm, g_hbm, out_ref, gi_ref, gk_ref,
    vol_ref, w_ref, g_ref, blocks, gpad, v3, vt, part, got,
    in_sem, z_send, z_recv, p_send, p_recv, r_send, r_recv, k_send, k_recv,
    *, scale,
):
    chans, count_s, count_h = lax.axis_size("chan"), lax.axis_size("sx"), lax.axis_size("sy")
    c, s, h = lax.axis_index("chan"), lax.axis_index("sx"), lax.axis_index("sy")
    rows_y, size_z, ch = vol_ref.shape[1:]
    half = rows_y // 2
    cells = half * size_z
    total = w_ref.shape[2]
    wide = 3 * ch
    core, far_s, far_h = s + 1 - 2 * (s % 2), (s + 2) % 4, 1 - h
    others = (c + 1 - 2 * (c % 2), (c + 2) % 4, 3 - c)
    to_x, to_y, to_core = {"sx": far_s}, {"sy": far_h}, {"sx": core}
    sent = []

    def remote(src, dst, send, recv, where):
        return pltpu.make_async_remote_copy(
            src_ref=src, dst_ref=dst, send_sem=send, recv_sem=recv,
            device_id=where, device_id_type=MESH,
        )

    def push(src, send, recv, where, dst=None):
        copy = remote(src, src if dst is None else dst, send, recv, where)
        copy.start()
        sent.append(copy)

    def arrived(ref, send, recv, where):
        remote(ref, ref, send, recv, where).wait_recv()

    loads = [
        pltpu.make_async_copy(src, dst, in_sem.at[k])
        for k, (src, dst) in enumerate(((g_hbm, g_ref), (vol_hbm, vol_ref), (w_hbm, w_ref)))
    ]
    for load in loads:
        load.start()
    barrier = pltpu.get_barrier_semaphore()
    partners = [{"chan": d} for d in others] + [to_x, to_y, to_core]
    for where in partners:
        pl.semaphore_signal(barrier, inc=1, device_id=where, device_id_type=MESH)

    zero_row = jnp.zeros((2, size_z, total // 2), BF16)
    zero_v = jnp.zeros((size_z, wide), BF16)
    last_x, last_y = v3.shape[0] - 1, v3.shape[1] - 1

    @pl.loop(0, last_y + 1)
    def _(y):
        for x in (0, last_x):
            gpad[:, x, y] = zero_row
            v3[x, y] = zero_v

    for x in range(1, last_x):
        for y in (0, last_y):
            gpad[:, x, y] = zero_row
            v3[x, y] = zero_v

    loads[0].wait()
    loads[1].wait()
    for index, ref in ((c, g_ref), (chans, vol_ref)):
        blocks[index, s, h, :, :, :ch] = ref[0, :half]
        blocks[index, s, h, :, :, ch:] = ref[0, half:]

    pl.semaphore_wait(barrier, len(partners))

    def offer(k, index):
        own = blocks.at[index, s, h]
        push(own, p_send.at[k, 0], p_recv.at[k, 0], to_x)
        push(own, p_send.at[k, 1], p_recv.at[k, 1], to_y)
        push(own, p_send.at[k, 2], p_recv.at[k, 2], to_core)

    def relay(k, index):
        from_x, from_y = blocks.at[index, far_s, h], blocks.at[index, s, far_h]
        cut = half // 2
        arrived(from_x, p_send.at[k, 0], p_recv.at[k, 0], to_x)
        push(from_x.at[:cut], p_send.at[k, 3], p_recv.at[k, 3], to_y)
        push(from_x, p_send.at[k, 5], p_recv.at[k, 5], to_core)
        arrived(from_y, p_send.at[k, 1], p_recv.at[k, 1], to_y)
        push(from_y.at[cut:], p_send.at[k, 4], p_recv.at[k, 4], to_x)
        push(from_y, p_send.at[k, 6], p_recv.at[k, 6], to_core)

    def corner(k, index):
        diag = blocks.at[index, far_s, far_h]
        cut = half // 2
        arrived(diag.at[:cut], p_send.at[k, 3], p_recv.at[k, 3], to_y)
        arrived(diag.at[cut:], p_send.at[k, 4], p_recv.at[k, 4], to_x)
        push(diag, p_send.at[k, 7], p_recv.at[k, 7], to_core)

    def from_core(k, index):
        far_core = 3 - s
        arrived(blocks.at[index, core, h], p_send.at[k, 2], p_recv.at[k, 2], to_core)
        arrived(blocks.at[index, far_core, h], p_send.at[k, 5], p_recv.at[k, 5], to_core)
        arrived(blocks.at[index, core, far_h], p_send.at[k, 6], p_recv.at[k, 6], to_core)
        arrived(blocks.at[index, far_core, far_h], p_send.at[k, 7], p_recv.at[k, 7], to_core)

    def from_chan(j):
        index = others[j]
        arrived(blocks.at[index, s, h], z_send.at[j], z_recv.at[j], {"chan": index})
        offer(j + 2, index)

    offer(0, chans)
    for j, d in enumerate(others):
        push(blocks.at[c, s, h], z_send.at[j], z_recv.at[j], {"chan": d})
    offer(1, c)

    relay(0, chans)
    relay(1, c)
    corner(0, chans)
    from_chan(0)
    corner(1, c)
    from_core(0, chans)
    relay(2, others[0])
    from_chan(1)

    row = lax.broadcasted_iota(jnp.int32, (cells, 2 * ch), 0) % size_z

    def shifted(x, hy):
        centre = blocks[chans, x, hy].reshape(cells, 2 * ch).astype(F32)
        before = jnp.where(row == 0, 0.0, pltpu.roll(centre, 1, 0))
        after = jnp.where(row == size_z - 1, 0.0, pltpu.roll(centre, cells - 1, 0))
        return before.astype(BF16), centre.astype(BF16), after.astype(BF16)

    @pl.loop(0, count_s * count_h)
    def _(n):
        x, hy = n // count_h, n % count_h
        parts = [moved.reshape(half, size_z, 2 * ch) for moved in shifted(x, hy)]
        for k in range(2):
            v3[x + 1, pl.ds(1 + hy * rows_y + k * half, half)] = jnp.concatenate(
                [moved[:, :, k * ch : (k + 1) * ch] for moved in parts], axis=-1
            )

    corner(2, others[0])
    relay(3, others[1])
    from_chan(2)
    loads[2].wait()

    for t in range(2):
        acc = jnp.zeros((cells, total), F32)
        for a in range(3):
            for b in range(3):
                window = v3[s + a, pl.ds(h * rows_y + t * half + b, half)].reshape(cells, wide)
                acc = acc + jnp.dot(window, w_ref[3 * a + b], preferred_element_type=F32)
        part[t] = acc

    for d in range(chans):
        for k in range(2):
            got[chans + d, :, k * ch : (k + 1) * ch] = part[k, :, d * ch : (d + 1) * ch]

    for j, d in enumerate(others):
        push(got.at[chans + d], r_send.at[j], r_recv.at[j], {"chan": d}, dst=got.at[c])

    corner(3, others[1])
    relay(4, others[2])

    @pl.loop(0, count_s * count_h)
    def _(n):
        x, hy = n // count_h, n % count_h
        for e, moved in enumerate(shifted(x, hy)):
            turned = moved.T
            for k in range(2):
                at = pl.multiple_of((hy * 2 + k) * cells, cells)
                vt[x, e * ch : (e + 1) * ch, pl.ds(at, cells)] = turned[k * ch : (k + 1) * ch]

    corner(4, others[2])

    def fill(pair):
        @pl.loop(0, count_s * count_h)
        def _(n):
            x, hy = n // count_h, n % count_h
            one, two = blocks[2 * pair, x, hy], blocks[2 * pair + 1, x, hy]
            for k in range(2):
                lanes = slice(k * ch, (k + 1) * ch)
                gpad[pair, x + 1, pl.ds(1 + hy * rows_y + k * half, half)] = jnp.concatenate(
                    [one[:, :, lanes], two[:, :, lanes]], axis=-1
                )

    from_core(1, c)
    from_core(2, others[0])
    fill(c // 2)
    from_core(3, others[1])
    from_core(4, others[2])
    fill(1 - c // 2)

    def cotangent(x, start, rows):
        return jnp.concatenate(
            [gpad[p, x, pl.ds(start, rows)].reshape(rows * size_z, total // 2) for p in range(2)],
            axis=-1,
        )

    core_at = s % 2
    all_y = rows_y * count_h
    top = wide // 2

    def weight_gradient(step, index, terms, at, rows):
        acc = jnp.zeros((rows, total), F32)
        for x_in, x_out, start in terms:
            acc = acc + jnp.dot(
                vt[x_in, pl.ds(at, rows), :], cotangent(x_out, start, all_y),
                preferred_element_type=F32,
            )
        gk_ref[index, pl.ds(at, rows)] = acc / scale
        push(gk_ref.at[index, pl.ds(at, rows)], k_send.at[step], k_recv.at[step], to_core)

    for b in range(3):
        weight_gradient(
            b, 6 * core_at + b,
            [(x + core_at, x + 2 - core_at, 2 - b) for x in range(count_s - 1)], 0, wide,
        )
    weight_gradient(
        3, 3 + 2 * core_at, [(x, x + 1, 2 - 2 * core_at) for x in range(count_s)], 0, wide
    )
    weight_gradient(
        4, 4, [(x, x + 1, 1) for x in range(count_s)], pl.multiple_of(core_at * top, top), top
    )

    row_out = lax.broadcasted_iota(jnp.int32, (cells, ch), 0) % size_z
    for t in range(2):
        acc = jnp.zeros((cells, wide), F32)
        for a in range(3):
            for b in range(3):
                window = cotangent(s + 2 - a, h * rows_y + t * half + 2 - b, half)
                acc = acc + lax.dot_general(
                    window, w_ref[3 * a + b],
                    (((1,), (1,)), ((), ())), preferred_element_type=F32,
                )
        first, middle, final = acc[:, :ch], acc[:, ch : 2 * ch], acc[:, 2 * ch :]
        later = jnp.where(row_out == size_z - 1, 0.0, pltpu.roll(first, cells - 1, 0))
        sooner = jnp.where(row_out == 0, 0.0, pltpu.roll(final, 1, 0))
        gi_ref[0, pl.ds(t * half, half)] = (
            (later + middle + sooner).astype(BF16).reshape(half, size_z, ch)
        )

    for j, d in enumerate(others):
        arrived(got.at[d], r_send.at[j], r_recv.at[j], {"chan": d})
    summed = got[chans + c]
    for d in others:
        summed = summed + got[d]
    narrow = summed.astype(BF16).reshape(half, size_z, 2 * ch)
    out_ref[0, :half] = narrow[:, :, :ch]
    out_ref[0, half:] = narrow[:, :, ch:]

    for b in range(3):
        arrived(gk_ref.at[6 * (1 - core_at) + b], k_send.at[b], k_recv.at[b], to_core)
    arrived(gk_ref.at[5 - 2 * core_at], k_send.at[3], k_recv.at[3], to_core)
    below = pl.multiple_of((1 - core_at) * top, top)
    arrived(gk_ref.at[4, pl.ds(below, top)], k_send.at[4], k_recv.at[4], to_core)
    for copy in sent:
        copy.wait_send()


def fused_body(volume, kernel, grad_out):
    chans, count_s, count_h = lax.axis_size("chan"), lax.axis_size("sx"), lax.axis_size("sy")
    _, rows_y, size_z, ch = volume.shape
    total = kernel.shape[2]
    half, wide = rows_y // 2, 3 * ch
    cells = half * size_z
    all_y = rows_y * count_h
    scale = math.sqrt(count_s * all_y * size_z)
    weights = kernel.reshape(9, wide, total)
    vmem = pl.BlockSpec(memory_space=pltpu.VMEM)
    dma = pltpu.SemaphoreType.DMA
    out, gi, gk = pl.pallas_call(
        functools.partial(fused_kernel, scale=scale),
        out_shape=(
            jax.ShapeDtypeStruct(volume.shape, BF16),
            jax.ShapeDtypeStruct(volume.shape, BF16),
            jax.ShapeDtypeStruct(weights.shape, F32),
        ),
        in_specs=[pl.BlockSpec(memory_space=pltpu.MemorySpace.HBM)] * 3,
        out_specs=(vmem,) * 3,
        scratch_shapes=[
            pltpu.VMEM(volume.shape, BF16),
            pltpu.VMEM(weights.shape, BF16),
            pltpu.VMEM(grad_out.shape, BF16),
            pltpu.VMEM((chans + 1, count_s, count_h, half, size_z, 2 * ch), BF16),
            pltpu.VMEM((2, count_s + 2, all_y + 2, size_z, total // 2), BF16),
            pltpu.VMEM((count_s + 2, all_y + 2, size_z, wide), BF16),
            pltpu.VMEM((count_s, wide, 2 * count_h * cells), BF16),
            pltpu.VMEM((2, cells, total), F32),
            pltpu.VMEM((2 * chans, cells, 2 * ch), F32),
            dma((3,)),
            dma((chans - 1,)), dma((chans - 1,)),
            dma((chans + 1, 8)), dma((chans + 1, 8)),
            dma((chans - 1,)), dma((chans - 1,)),
            dma((5,)), dma((5,)),
        ],
        compiler_params=pltpu.CompilerParams(
            collective_id=0, has_side_effects=True, vmem_limit_bytes=50 * 2**20
        ),
    )(volume, weights, grad_out)
    return out, gi, gk.reshape(kernel.shape)


def solution(mesh):
    small = (mesh.shape["chan"], mesh.shape["sx"], mesh.shape["sy"]) == (4, 4, 2)
    return jax.shard_map(
        fused_body if small else body,
        mesh=mesh,
        in_specs=(P("sx", "sy", None, "chan"), P(None, "chan", None), P("sx", "sy", None, "chan")),
        out_specs=(P("sx", "sy", None, "chan"), P("sx", "sy", None, "chan"), P(None, "chan", None)),
        check_vma=False,
    )
```

```python
import functools
import math

import jax
import jax.numpy as jnp
from jax import lax
from jax.experimental import pallas as pl
from jax.experimental.pallas import tpu as pltpu
from jax.sharding import PartitionSpec as P


def padded_2(shard, sides, width):
    for axis, dim in sides:
        count, length = (lax.axis_size(axis), shard.shape[dim])
        up = [(i, (i + 1) % count) for i in range(count - 1)]
        down = [(j, i) for i, j in up]
        last = lax.slice_in_dim(shard, length - width, length, axis=dim)
        leading = lax.slice_in_dim(shard, 0, width, axis=dim)
        before = lax.ppermute(last, axis, up)
        after = lax.ppermute(leading, axis, down)
        shard = jnp.concatenate([before, shard, after], axis=dim)
    return shard


def body(volume, kernel, grad_out):
    size_x, size_y, size_z, own_in = volume.shape
    total_out = kernel.shape[2]
    cells = size_x * size_y * size_z
    rim = padded_2(volume, (("sx", 0), ("sy", 1)), 1)
    padded = jnp.pad(rim, ((0, 0), (0, 0), (1, 1), (0, 0)))
    offsets = [(index // 9, index // 3 % 3, index % 3) for index in range(27)]
    partial_out = jnp.zeros((cells, total_out), jnp.float32)
    for index in range(27):
        a, b, e = offsets[index]
        window = padded[a : a + size_x, b : b + size_y, e : e + size_z].reshape(cells, own_in)
        partial_out = partial_out + jnp.dot(
            window, kernel[index], preferred_element_type=jnp.float32
        )
    partial_out = partial_out.reshape(size_x, size_y, size_z, total_out)
    out = lax.psum_scatter(partial_out, "chan", scatter_dimension=3, tiled=True).astype(
        jnp.bfloat16
    )
    grad_full = lax.all_gather(grad_out, "chan", axis=3, tiled=True)
    grad_rimmed = padded_2(grad_full, (("sx", 0), ("sy", 1)), 1)
    grad_padded = jnp.pad(grad_rimmed, ((0, 0), (0, 0), (1, 1), (0, 0)))
    flat_grad = grad_full.reshape(cells, total_out)
    back = jnp.zeros((cells, own_in), jnp.float32)
    kernel_terms = []
    for index in range(27):
        a, b, e = offsets[index]
        window = grad_padded[
            2 - a : 2 - a + size_x, 2 - b : 2 - b + size_y, 2 - e : 2 - e + size_z
        ].reshape(cells, total_out)
        back = back + lax.dot_general(
            window, kernel[index], (((1,), (1,)), ((), ())), preferred_element_type=jnp.float32
        )
        in_window = padded[a : a + size_x, b : b + size_y, e : e + size_z].reshape(cells, own_in)
        kernel_terms.append(
            lax.dot_general(
                in_window, flat_grad, (((0,), (0,)), ((), ())), preferred_element_type=jnp.float32
            )
        )
    grad_input = back.reshape(size_x, size_y, size_z, own_in).astype(jnp.bfloat16)
    local_kernel = jnp.stack(kernel_terms)
    summed = lax.psum(local_kernel, ("sx", "sy"))
    all_cells = cells * lax.axis_size("sx") * lax.axis_size("sy")
    grad_kernel = summed / jnp.float32(math.sqrt(all_cells))
    return (out, grad_input, grad_kernel)


MESH = pl.DeviceIdType.MESH
F32 = jnp.float32
BF16 = jnp.bfloat16


def fused_kernel(
    vol_hbm, w_hbm, g_hbm, out_ref, gi_ref, gk_ref,
    vol_ref, w_ref, g_ref, blocks, gpad, v3, vt, part, got,
    in_sem, z_send, z_recv, p_send, p_recv, r_send, r_recv, k_send, k_recv,
    *, scale,
):
    chans, count_s, count_h = lax.axis_size("chan"), lax.axis_size("sx"), lax.axis_size("sy")
    c, s, h = lax.axis_index("chan"), lax.axis_index("sx"), lax.axis_index("sy")
    rows_y, size_z, ch = vol_ref.shape[1:]
    half = rows_y // 2
    cells = half * size_z
    total = w_ref.shape[2]
    wide = 3 * ch
    core, far_s, far_h = s + 1 - 2 * (s % 2), (s + 2) % 4, 1 - h
    others = (c + 1 - 2 * (c % 2), (c + 2) % 4, 3 - c)
    to_x, to_y, to_core = {"sx": far_s}, {"sy": far_h}, {"sx": core}
    sent = []

    def remote(src, dst, send, recv, where):
        return pltpu.make_async_remote_copy(
            src_ref=src, dst_ref=dst, send_sem=send, recv_sem=recv,
            device_id=where, device_id_type=MESH,
        )

    def push(src, send, recv, where, dst=None):
        copy = remote(src, src if dst is None else dst, send, recv, where)
        copy.start()
        sent.append(copy)

    def arrived(ref, send, recv, where):
        remote(ref, ref, send, recv, where).wait_recv()

    loads = [
        pltpu.make_async_copy(src, dst, in_sem.at[k])
        for k, (src, dst) in enumerate(((g_hbm, g_ref), (vol_hbm, vol_ref), (w_hbm, w_ref)))
    ]
    for load in loads:
        load.start()
    barrier = pltpu.get_barrier_semaphore()
    partners = [{"chan": d} for d in others] + [to_x, to_y, to_core]
    for where in partners:
        pl.semaphore_signal(barrier, inc=1, device_id=where, device_id_type=MESH)

    zero_row = jnp.zeros((2, size_z, total // 2), BF16)
    last_x, last_y = gpad.shape[1] - 1, gpad.shape[2] - 1

    @pl.loop(0, last_y + 1)
    def _(y):
        for x in (0, last_x):
            gpad[:, x, y] = zero_row

    for x in range(1, last_x):
        for y in (0, last_y):
            gpad[:, x, y] = zero_row
    v3[...] = jnp.zeros(v3.shape, BF16)

    loads[0].wait()
    loads[1].wait()
    for index, ref in ((c, g_ref), (chans, vol_ref)):
        blocks[index, s, h, :, :, :ch] = ref[0, :half]
        blocks[index, s, h, :, :, ch:] = ref[0, half:]

    pl.semaphore_wait(barrier, len(partners))

    def offer(k, index):
        own = blocks.at[index, s, h]
        push(own, p_send.at[k, 0], p_recv.at[k, 0], to_x)
        push(own, p_send.at[k, 1], p_recv.at[k, 1], to_y)
        push(own, p_send.at[k, 2], p_recv.at[k, 2], to_core)

    def relay(k, index):
        from_x, from_y = blocks.at[index, far_s, h], blocks.at[index, s, far_h]
        cut = half // 2
        arrived(from_x, p_send.at[k, 0], p_recv.at[k, 0], to_x)
        push(from_x.at[:cut], p_send.at[k, 3], p_recv.at[k, 3], to_y)
        push(from_x, p_send.at[k, 5], p_recv.at[k, 5], to_core)
        arrived(from_y, p_send.at[k, 1], p_recv.at[k, 1], to_y)
        push(from_y.at[cut:], p_send.at[k, 4], p_recv.at[k, 4], to_x)
        push(from_y, p_send.at[k, 6], p_recv.at[k, 6], to_core)

    def corner(k, index):
        diag = blocks.at[index, far_s, far_h]
        cut = half // 2
        arrived(diag.at[:cut], p_send.at[k, 3], p_recv.at[k, 3], to_y)
        arrived(diag.at[cut:], p_send.at[k, 4], p_recv.at[k, 4], to_x)
        push(diag, p_send.at[k, 7], p_recv.at[k, 7], to_core)

    def from_core(k, index):
        far_core = 3 - s
        arrived(blocks.at[index, core, h], p_send.at[k, 2], p_recv.at[k, 2], to_core)
        arrived(blocks.at[index, far_core, h], p_send.at[k, 5], p_recv.at[k, 5], to_core)
        arrived(blocks.at[index, core, far_h], p_send.at[k, 6], p_recv.at[k, 6], to_core)
        arrived(blocks.at[index, far_core, far_h], p_send.at[k, 7], p_recv.at[k, 7], to_core)

    def from_chan(j):
        index = others[j]
        arrived(blocks.at[index, s, h], z_send.at[j], z_recv.at[j], {"chan": index})
        offer(j + 2, index)

    offer(0, chans)
    for j, d in enumerate(others):
        push(blocks.at[c, s, h], z_send.at[j], z_recv.at[j], {"chan": d})
    offer(1, c)

    def shifted(block):
        wide_block = block.astype(F32)
        row = lax.broadcasted_iota(jnp.int32, block.shape, 0) % size_z
        before = jnp.where(row == 0, 0.0, pltpu.roll(wide_block, 1, 0))
        after = jnp.where(row == size_z - 1, 0.0, pltpu.roll(wide_block, block.shape[0] - 1, 0))
        return before.astype(BF16), block, after.astype(BF16)

    def spread(dx, x):
        parts = shifted(blocks[chans, x, h].reshape(cells, 2 * ch))
        parts = [moved.reshape(half, size_z, 2 * ch) for moved in parts]
        for k in range(2):
            v3[dx, 1 + k * half : 1 + (k + 1) * half] = jnp.concatenate(
                [moved[:, :, k * ch : (k + 1) * ch] for moved in parts], axis=-1
            )

    def spread_edge(dx, x):
        for side, (piece, lanes, row_at) in enumerate(
            ((0, slice(0, ch), rows_y + 1), (half - 1, slice(ch, 2 * ch), 0))
        ):
            @pl.when(h == side)
            def _():
                parts = shifted(blocks[chans, x, 1 - side, piece])
                v3[dx, row_at] = jnp.concatenate([moved[:, lanes] for moved in parts], axis=-1)

    spread(1, s)
    relay(0, chans)
    relay(1, c)
    corner(0, chans)
    from_core(0, chans)
    spread_edge(1, s)
    for dx in (0, 2):
        @pl.when((s + dx >= 1) & (s + dx <= count_s))
        def _():
            spread(dx, s + dx - 1)
            spread_edge(dx, s + dx - 1)

    from_chan(0)
    corner(1, c)
    loads[2].wait()

    acc = jnp.zeros((2 * cells, total), F32)
    for a in range(3):
        for b in range(3):
            window = v3[a, b : b + rows_y].reshape(2 * cells, wide)
            acc = acc + jnp.dot(window, w_ref[3 * a + b], preferred_element_type=F32)
    part[...] = acc.reshape(2, cells, total)

    for d in range(chans):
        for k in range(2):
            got[chans + d, :, k * ch : (k + 1) * ch] = part[k, :, d * ch : (d + 1) * ch]

    for j, d in enumerate(others):
        push(got.at[chans + d], r_send.at[j], r_recv.at[j], {"chan": d}, dst=got.at[c])

    relay(2, others[0])
    from_chan(1)
    corner(2, others[0])
    from_chan(2)
    relay(3, others[1])

    def turn(n):
        x, hy = n // count_h, n % count_h
        for e, moved in enumerate(shifted(blocks[chans, x, hy].reshape(cells, 2 * ch))):
            turned = moved.T
            for k in range(2):
                at = pl.multiple_of((hy * 2 + k) * cells, cells)
                vt[x, e * ch : (e + 1) * ch, pl.ds(at, cells)] = turned[k * ch : (k + 1) * ch]

    turns = count_s * count_h
    pl.loop(0, turns // 4)(turn)
    corner(3, others[1])
    relay(4, others[2])
    pl.loop(turns // 4, turns // 2)(turn)
    corner(4, others[2])
    pl.loop(turns // 2, turns)(turn)

    def fill(pair):
        @pl.loop(0, count_s * count_h)
        def _(n):
            x, hy = n // count_h, n % count_h
            one, two = blocks[2 * pair, x, hy], blocks[2 * pair + 1, x, hy]
            for k in range(2):
                lanes = slice(k * ch, (k + 1) * ch)
                gpad[pair, x + 1, pl.ds(1 + hy * rows_y + k * half, half)] = jnp.concatenate(
                    [one[:, :, lanes], two[:, :, lanes]], axis=-1
                )

    from_core(1, c)
    from_core(2, others[0])
    fill(c // 2)
    from_core(3, others[1])
    from_core(4, others[2])
    fill(1 - c // 2)

    def cotangent(x, start, rows):
        return jnp.concatenate(
            [gpad[p, x, pl.ds(start, rows)].reshape(rows * size_z, total // 2) for p in range(2)],
            axis=-1,
        )

    core_at = s % 2
    all_y = rows_y * count_h
    top = wide // 2

    def weight_gradient(step, index, terms, at, rows):
        acc = jnp.zeros((rows, total), F32)
        for x_in, x_out, start in terms:
            acc = acc + jnp.dot(
                vt[x_in, pl.ds(at, rows), :], cotangent(x_out, start, all_y),
                preferred_element_type=F32,
            )
        gk_ref[index, pl.ds(at, rows)] = acc / scale
        push(gk_ref.at[index, pl.ds(at, rows)], k_send.at[step], k_recv.at[step], to_core)

    for b in range(3):
        weight_gradient(
            b, 6 * core_at + b,
            [(x + core_at, x + 2 - core_at, 2 - b) for x in range(count_s - 1)], 0, wide,
        )
    weight_gradient(
        3, 3 + 2 * core_at, [(x, x + 1, 2 - 2 * core_at) for x in range(count_s)], 0, wide
    )
    weight_gradient(
        4, 4, [(x, x + 1, 1) for x in range(count_s)], pl.multiple_of(core_at * top, top), top
    )

    row_out = lax.broadcasted_iota(jnp.int32, (2 * cells, ch), 0) % size_z
    acc = jnp.zeros((2 * cells, wide), F32)
    for a in range(3):
        for b in range(3):
            acc = acc + lax.dot_general(
                cotangent(s + 2 - a, h * rows_y + 2 - b, rows_y), w_ref[3 * a + b],
                (((1,), (1,)), ((), ())), preferred_element_type=F32,
            )
    first, middle, final = acc[:, :ch], acc[:, ch : 2 * ch], acc[:, 2 * ch :]
    later = jnp.where(row_out == size_z - 1, 0.0, pltpu.roll(first, 2 * cells - 1, 0))
    sooner = jnp.where(row_out == 0, 0.0, pltpu.roll(final, 1, 0))
    gi_ref[0] = (later + middle + sooner).astype(BF16).reshape(rows_y, size_z, ch)

    for j, d in enumerate(others):
        arrived(got.at[d], r_send.at[j], r_recv.at[j], {"chan": d})
    summed = got[chans + c]
    for d in others:
        summed = summed + got[d]
    narrow = summed.astype(BF16).reshape(half, size_z, 2 * ch)
    out_ref[0, :half] = narrow[:, :, :ch]
    out_ref[0, half:] = narrow[:, :, ch:]

    for b in range(3):
        arrived(gk_ref.at[6 * (1 - core_at) + b], k_send.at[b], k_recv.at[b], to_core)
    arrived(gk_ref.at[5 - 2 * core_at], k_send.at[3], k_recv.at[3], to_core)
    below = pl.multiple_of((1 - core_at) * top, top)
    arrived(gk_ref.at[4, pl.ds(below, top)], k_send.at[4], k_recv.at[4], to_core)
    for copy in sent:
        copy.wait_send()


def fused_body(volume, kernel, grad_out):
    chans, count_s, count_h = lax.axis_size("chan"), lax.axis_size("sx"), lax.axis_size("sy")
    _, rows_y, size_z, ch = volume.shape
    total = kernel.shape[2]
    half, wide = rows_y // 2, 3 * ch
    cells = half * size_z
    all_y = rows_y * count_h
    scale = math.sqrt(count_s * all_y * size_z)
    weights = kernel.reshape(9, wide, total)
    vmem = pl.BlockSpec(memory_space=pltpu.VMEM)
    dma = pltpu.SemaphoreType.DMA
    out, gi, gk = pl.pallas_call(
        functools.partial(fused_kernel, scale=scale),
        out_shape=(
            jax.ShapeDtypeStruct(volume.shape, BF16),
            jax.ShapeDtypeStruct(volume.shape, BF16),
            jax.ShapeDtypeStruct(weights.shape, F32),
        ),
        in_specs=[pl.BlockSpec(memory_space=pltpu.MemorySpace.HBM)] * 3,
        out_specs=(vmem,) * 3,
        scratch_shapes=[
            pltpu.VMEM(volume.shape, BF16),
            pltpu.VMEM(weights.shape, BF16),
            pltpu.VMEM(grad_out.shape, BF16),
            pltpu.VMEM((chans + 1, count_s, count_h, half, size_z, 2 * ch), BF16),
            pltpu.VMEM((2, count_s + 2, all_y + 2, size_z, total // 2), BF16),
            pltpu.VMEM((3, rows_y + 2, size_z, wide), BF16),
            pltpu.VMEM((count_s, wide, 2 * count_h * cells), BF16),
            pltpu.VMEM((2, cells, total), F32),
            pltpu.VMEM((2 * chans, cells, 2 * ch), F32),
            dma((3,)),
            dma((chans - 1,)), dma((chans - 1,)),
            dma((chans + 1, 8)), dma((chans + 1, 8)),
            dma((chans - 1,)), dma((chans - 1,)),
            dma((5,)), dma((5,)),
        ],
        compiler_params=pltpu.CompilerParams(
            collective_id=0, has_side_effects=True, vmem_limit_bytes=60 * 2**20
        ),
    )(volume, weights, grad_out)
    return out, gi, gk.reshape(kernel.shape)


def solution(mesh):
    small = (mesh.shape["chan"], mesh.shape["sx"], mesh.shape["sy"]) == (4, 4, 2)
    return jax.shard_map(
        fused_body if small else body,
        mesh=mesh,
        in_specs=(P("sx", "sy", None, "chan"), P(None, "chan", None), P("sx", "sy", None, "chan")),
        out_specs=(P("sx", "sy", None, "chan"), P("sx", "sy", None, "chan"), P(None, "chan", None)),
        check_vma=False,
    )
```

```python
import functools
import math

import jax
import jax.numpy as jnp
from jax import lax
from jax.experimental import pallas as pl
from jax.experimental.pallas import tpu as pltpu
from jax.sharding import PartitionSpec as P


def padded_2(shard, sides, width):
    for axis, dim in sides:
        count, length = (lax.axis_size(axis), shard.shape[dim])
        up = [(i, (i + 1) % count) for i in range(count - 1)]
        down = [(j, i) for i, j in up]
        last = lax.slice_in_dim(shard, length - width, length, axis=dim)
        leading = lax.slice_in_dim(shard, 0, width, axis=dim)
        before = lax.ppermute(last, axis, up)
        after = lax.ppermute(leading, axis, down)
        shard = jnp.concatenate([before, shard, after], axis=dim)
    return shard


def body(volume, kernel, grad_out):
    size_x, size_y, size_z, own_in = volume.shape
    total_out = kernel.shape[2]
    cells = size_x * size_y * size_z
    rim = padded_2(volume, (("sx", 0), ("sy", 1)), 1)
    padded = jnp.pad(rim, ((0, 0), (0, 0), (1, 1), (0, 0)))
    offsets = [(index // 9, index // 3 % 3, index % 3) for index in range(27)]
    partial_out = jnp.zeros((cells, total_out), jnp.float32)
    for index in range(27):
        a, b, e = offsets[index]
        window = padded[a : a + size_x, b : b + size_y, e : e + size_z].reshape(cells, own_in)
        partial_out = partial_out + jnp.dot(
            window, kernel[index], preferred_element_type=jnp.float32
        )
    partial_out = partial_out.reshape(size_x, size_y, size_z, total_out)
    out = lax.psum_scatter(partial_out, "chan", scatter_dimension=3, tiled=True).astype(
        jnp.bfloat16
    )
    grad_full = lax.all_gather(grad_out, "chan", axis=3, tiled=True)
    grad_rimmed = padded_2(grad_full, (("sx", 0), ("sy", 1)), 1)
    grad_padded = jnp.pad(grad_rimmed, ((0, 0), (0, 0), (1, 1), (0, 0)))
    flat_grad = grad_full.reshape(cells, total_out)
    back = jnp.zeros((cells, own_in), jnp.float32)
    kernel_terms = []
    for index in range(27):
        a, b, e = offsets[index]
        window = grad_padded[
            2 - a : 2 - a + size_x, 2 - b : 2 - b + size_y, 2 - e : 2 - e + size_z
        ].reshape(cells, total_out)
        back = back + lax.dot_general(
            window, kernel[index], (((1,), (1,)), ((), ())), preferred_element_type=jnp.float32
        )
        in_window = padded[a : a + size_x, b : b + size_y, e : e + size_z].reshape(cells, own_in)
        kernel_terms.append(
            lax.dot_general(
                in_window, flat_grad, (((0,), (0,)), ((), ())), preferred_element_type=jnp.float32
            )
        )
    grad_input = back.reshape(size_x, size_y, size_z, own_in).astype(jnp.bfloat16)
    local_kernel = jnp.stack(kernel_terms)
    summed = lax.psum(local_kernel, ("sx", "sy"))
    all_cells = cells * lax.axis_size("sx") * lax.axis_size("sy")
    grad_kernel = summed / jnp.float32(math.sqrt(all_cells))
    return (out, grad_input, grad_kernel)


MESH = pl.DeviceIdType.MESH
F32 = jnp.float32
BF16 = jnp.bfloat16


def shifted(block, size_z):
    wide_block = block.astype(F32)
    row = lax.broadcasted_iota(jnp.int32, block.shape, 0) % size_z
    before = jnp.where(row == 0, 0.0, pltpu.roll(wide_block, 1, 0))
    after = jnp.where(row == size_z - 1, 0.0, pltpu.roll(wide_block, block.shape[0] - 1, 0))
    return before.astype(BF16), block, after.astype(BF16)


def gather_kernel(
    vol_hbm, w_hbm, g_hbm, out_ref, blocks,
    vol_ref, w_ref, g_ref, v3, part, got,
    in_sem, z_send, z_recv, p_send, p_recv, r_send, r_recv,
):
    chans, count_s, count_h = lax.axis_size("chan"), lax.axis_size("sx"), lax.axis_size("sy")
    c, s, h = lax.axis_index("chan"), lax.axis_index("sx"), lax.axis_index("sy")
    rows_y, size_z, ch = vol_ref.shape[1:]
    half = rows_y // 2
    cells = half * size_z
    total = w_ref.shape[2]
    wide = 3 * ch
    core, far_s, far_h = s + 1 - 2 * (s % 2), (s + 2) % 4, 1 - h
    others = (c + 1 - 2 * (c % 2), (c + 2) % 4, 3 - c)
    to_x, to_y, to_core = {"sx": far_s}, {"sy": far_h}, {"sx": core}
    sent = []

    def remote(src, dst, send, recv, where):
        return pltpu.make_async_remote_copy(
            src_ref=src, dst_ref=dst, send_sem=send, recv_sem=recv,
            device_id=where, device_id_type=MESH,
        )

    def push(src, send, recv, where, dst=None):
        copy = remote(src, src if dst is None else dst, send, recv, where)
        copy.start()
        sent.append(copy)

    def arrived(ref, send, recv, where):
        remote(ref, ref, send, recv, where).wait_recv()

    loads = [
        pltpu.make_async_copy(src, dst, in_sem.at[k])
        for k, (src, dst) in enumerate(((g_hbm, g_ref), (vol_hbm, vol_ref), (w_hbm, w_ref)))
    ]
    for load in loads:
        load.start()
    barrier = pltpu.get_barrier_semaphore()
    partners = [{"chan": d} for d in others] + [to_x, to_y, to_core]
    for where in partners:
        pl.semaphore_signal(barrier, inc=1, device_id=where, device_id_type=MESH)

    v3[...] = jnp.zeros(v3.shape, BF16)

    loads[0].wait()
    loads[1].wait()
    for index, ref in ((c, g_ref), (chans, vol_ref)):
        blocks[index, s, h, :, :, :ch] = ref[0, :half]
        blocks[index, s, h, :, :, ch:] = ref[0, half:]

    pl.semaphore_wait(barrier, len(partners))

    def offer(k, index):
        own = blocks.at[index, s, h]
        push(own, p_send.at[k, 0], p_recv.at[k, 0], to_x)
        push(own, p_send.at[k, 1], p_recv.at[k, 1], to_y)
        push(own, p_send.at[k, 2], p_recv.at[k, 2], to_core)

    def relay(k, index):
        from_x, from_y = blocks.at[index, far_s, h], blocks.at[index, s, far_h]
        cut = half // 2
        arrived(from_x, p_send.at[k, 0], p_recv.at[k, 0], to_x)
        push(from_x.at[:cut], p_send.at[k, 3], p_recv.at[k, 3], to_y)
        push(from_x, p_send.at[k, 5], p_recv.at[k, 5], to_core)
        arrived(from_y, p_send.at[k, 1], p_recv.at[k, 1], to_y)
        push(from_y.at[cut:], p_send.at[k, 4], p_recv.at[k, 4], to_x)
        push(from_y, p_send.at[k, 6], p_recv.at[k, 6], to_core)

    def corner(k, index):
        diag = blocks.at[index, far_s, far_h]
        cut = half // 2
        arrived(diag.at[:cut], p_send.at[k, 3], p_recv.at[k, 3], to_y)
        arrived(diag.at[cut:], p_send.at[k, 4], p_recv.at[k, 4], to_x)
        push(diag, p_send.at[k, 7], p_recv.at[k, 7], to_core)

    def from_core(k, index):
        far_core = 3 - s
        arrived(blocks.at[index, core, h], p_send.at[k, 2], p_recv.at[k, 2], to_core)
        arrived(blocks.at[index, far_core, h], p_send.at[k, 5], p_recv.at[k, 5], to_core)
        arrived(blocks.at[index, core, far_h], p_send.at[k, 6], p_recv.at[k, 6], to_core)
        arrived(blocks.at[index, far_core, far_h], p_send.at[k, 7], p_recv.at[k, 7], to_core)

    def from_chan(j):
        index = others[j]
        arrived(blocks.at[index, s, h], z_send.at[j], z_recv.at[j], {"chan": index})
        offer(j + 2, index)

    offer(0, chans)
    for j, d in enumerate(others):
        push(blocks.at[c, s, h], z_send.at[j], z_recv.at[j], {"chan": d})
    offer(1, c)

    def spread(dx, x):
        parts = shifted(blocks[chans, x, h].reshape(cells, 2 * ch), size_z)
        parts = [moved.reshape(half, size_z, 2 * ch) for moved in parts]
        for k in range(2):
            v3[dx, 1 + k * half : 1 + (k + 1) * half] = jnp.concatenate(
                [moved[:, :, k * ch : (k + 1) * ch] for moved in parts], axis=-1
            )

    def spread_edge(dx, x):
        for side, (piece, lanes, row_at) in enumerate(
            ((0, slice(0, ch), rows_y + 1), (half - 1, slice(ch, 2 * ch), 0))
        ):
            @pl.when(h == side)
            def _():
                parts = shifted(blocks[chans, x, 1 - side, piece], size_z)
                v3[dx, row_at] = jnp.concatenate([moved[:, lanes] for moved in parts], axis=-1)

    spread(1, s)
    relay(0, chans)
    relay(1, c)
    corner(0, chans)
    from_core(0, chans)
    spread_edge(1, s)
    for dx in (0, 2):
        @pl.when((s + dx >= 1) & (s + dx <= count_s))
        def _():
            spread(dx, s + dx - 1)
            spread_edge(dx, s + dx - 1)

    from_chan(0)
    corner(1, c)
    loads[2].wait()

    acc = jnp.zeros((2 * cells, total), F32)
    for a in range(3):
        for b in range(3):
            window = v3[a, b : b + rows_y].reshape(2 * cells, wide)
            acc = acc + jnp.dot(window, w_ref[3 * a + b], preferred_element_type=F32)
    part[...] = acc.reshape(2, cells, total)

    for d in range(chans):
        for k in range(2):
            got[chans + d, :, k * ch : (k + 1) * ch] = part[k, :, d * ch : (d + 1) * ch]

    for j, d in enumerate(others):
        push(got.at[chans + d], r_send.at[j], r_recv.at[j], {"chan": d}, dst=got.at[c])

    relay(2, others[0])
    from_chan(1)
    corner(2, others[0])
    from_chan(2)
    relay(3, others[1])

    corner(3, others[1])
    relay(4, others[2])
    corner(4, others[2])
    for k, index in enumerate((c,) + others):
        from_core(k + 1, index)

    for j, d in enumerate(others):
        arrived(got.at[d], r_send.at[j], r_recv.at[j], {"chan": d})
    summed = got[chans + c]
    for d in others:
        summed = summed + got[d]
    narrow = summed.astype(BF16).reshape(half, size_z, 2 * ch)
    out_ref[0, :half] = narrow[:, :, :ch]
    out_ref[0, half:] = narrow[:, :, ch:]

    for copy in sent:
        copy.wait_send()


def gradient_kernel(blocks, w_ref, gi_ref, gk_ref, gpad, vt, *, scale):
    chans, count_s, count_h = lax.axis_size("chan"), lax.axis_size("sx"), lax.axis_size("sy")
    s, h = lax.axis_index("sx"), lax.axis_index("sy")
    _, rows_y, size_z, ch = gi_ref.shape
    half = rows_y // 2
    cells = half * size_z
    total = w_ref.shape[2]
    wide = 3 * ch

    zero_row = jnp.zeros((2, size_z, total // 2), BF16)
    last_x, last_y = gpad.shape[1] - 1, gpad.shape[2] - 1

    @pl.loop(0, last_y + 1)
    def _(y):
        for x in (0, last_x):
            gpad[:, x, y] = zero_row

    for x in range(1, last_x):
        for y in (0, last_y):
            gpad[:, x, y] = zero_row
    def turn(n):
        x, hy = n // count_h, n % count_h
        for e, moved in enumerate(shifted(blocks[chans, x, hy].reshape(cells, 2 * ch), size_z)):
            turned = moved.T
            for k in range(2):
                at = pl.multiple_of((hy * 2 + k) * cells, cells)
                vt[x, e * ch : (e + 1) * ch, pl.ds(at, cells)] = turned[k * ch : (k + 1) * ch]

    pl.loop(0, count_s * count_h)(turn)

    def fill(pair):
        @pl.loop(0, count_s * count_h)
        def _(n):
            x, hy = n // count_h, n % count_h
            one, two = blocks[2 * pair, x, hy], blocks[2 * pair + 1, x, hy]
            for k in range(2):
                lanes = slice(k * ch, (k + 1) * ch)
                gpad[pair, x + 1, pl.ds(1 + hy * rows_y + k * half, half)] = jnp.concatenate(
                    [one[:, :, lanes], two[:, :, lanes]], axis=-1
                )

    fill(0)
    fill(1)

    def cotangent(x, start, rows):
        return jnp.concatenate(
            [gpad[p, x, pl.ds(start, rows)].reshape(rows * size_z, total // 2) for p in range(2)],
            axis=-1,
        )

    row_out = lax.broadcasted_iota(jnp.int32, (2 * cells, ch), 0) % size_z
    acc = jnp.zeros((2 * cells, wide), F32)
    for a in range(3):
        for b in range(3):
            acc = acc + lax.dot_general(
                cotangent(s + 2 - a, h * rows_y + 2 - b, rows_y), w_ref[3 * a + b],
                (((1,), (1,)), ((), ())), preferred_element_type=F32,
            )
    first, middle, final = acc[:, :ch], acc[:, ch : 2 * ch], acc[:, 2 * ch :]
    later = jnp.where(row_out == size_z - 1, 0.0, pltpu.roll(first, 2 * cells - 1, 0))
    sooner = jnp.where(row_out == 0, 0.0, pltpu.roll(final, 1, 0))
    gi_ref[0] = (later + middle + sooner).astype(BF16).reshape(rows_y, size_z, ch)

    all_y = rows_y * count_h
    for a in range(3):

        @pl.loop(0, 3)
        def _(b):
            acc = jnp.zeros((wide, total), F32)
            for x in range(count_s):
                if 0 <= x + 1 - a < count_s:
                    acc = acc + jnp.dot(
                        vt[x], cotangent(x + 2 - a, 2 - b, all_y), preferred_element_type=F32
                    )
            gk_ref[3 * a + b] = acc / scale


def fused_body(volume, kernel, grad_out):
    chans, count_s, count_h = lax.axis_size("chan"), lax.axis_size("sx"), lax.axis_size("sy")
    _, rows_y, size_z, ch = volume.shape
    total = kernel.shape[2]
    half, wide = rows_y // 2, 3 * ch
    cells = half * size_z
    all_y = rows_y * count_h
    scale = math.sqrt(count_s * all_y * size_z)
    weights = kernel.reshape(9, wide, total)
    vmem = pl.BlockSpec(memory_space=pltpu.VMEM)
    hbm = pl.BlockSpec(memory_space=pltpu.MemorySpace.HBM)
    dma = pltpu.SemaphoreType.DMA
    out, blocks = pl.pallas_call(
        gather_kernel,
        out_shape=(
            jax.ShapeDtypeStruct(volume.shape, BF16),
            jax.ShapeDtypeStruct((chans + 1, count_s, count_h, half, size_z, 2 * ch), BF16),
        ),
        in_specs=[hbm] * 3,
        out_specs=(vmem, vmem),
        scratch_shapes=[
            pltpu.VMEM(volume.shape, BF16),
            pltpu.VMEM(weights.shape, BF16),
            pltpu.VMEM(grad_out.shape, BF16),
            pltpu.VMEM((3, rows_y + 2, size_z, wide), BF16),
            pltpu.VMEM((2, cells, total), F32),
            pltpu.VMEM((2 * chans, cells, 2 * ch), F32),
            dma((3,)),
            dma((chans - 1,)), dma((chans - 1,)),
            dma((chans + 1, 8)), dma((chans + 1, 8)),
            dma((chans - 1,)), dma((chans - 1,)),
        ],
        compiler_params=pltpu.CompilerParams(
            collective_id=0, has_side_effects=True, vmem_limit_bytes=40 * 2**20
        ),
    )(volume, weights, grad_out)
    gi, gk = pl.pallas_call(
        functools.partial(gradient_kernel, scale=scale),
        out_shape=(
            jax.ShapeDtypeStruct(volume.shape, BF16),
            jax.ShapeDtypeStruct(weights.shape, F32),
        ),
        in_specs=[vmem] * 2,
        out_specs=(vmem, vmem),
        scratch_shapes=[
            pltpu.VMEM((2, count_s + 2, all_y + 2, size_z, total // 2), BF16),
            pltpu.VMEM((count_s, wide, 2 * count_h * cells), BF16),
        ],
        compiler_params=pltpu.CompilerParams(vmem_limit_bytes=40 * 2**20),
    )(blocks, weights)
    return out, gi, gk.reshape(kernel.shape)


def solution(mesh):
    small = (mesh.shape["chan"], mesh.shape["sx"], mesh.shape["sy"]) == (4, 4, 2)
    return jax.shard_map(
        fused_body if small else body,
        mesh=mesh,
        in_specs=(P("sx", "sy", None, "chan"), P(None, "chan", None), P("sx", "sy", None, "chan")),
        out_specs=(P("sx", "sy", None, "chan"), P("sx", "sy", None, "chan"), P(None, "chan", None)),
        check_vma=False,
    )
```

```python
import functools
import math

import jax
import jax.numpy as jnp
from jax import lax
from jax.experimental import pallas as pl
from jax.experimental.pallas import tpu as pltpu
from jax.sharding import PartitionSpec as P


def padded_2(shard, sides, width):
    for axis, dim in sides:
        count, length = (lax.axis_size(axis), shard.shape[dim])
        up = [(i, (i + 1) % count) for i in range(count - 1)]
        down = [(j, i) for i, j in up]
        last = lax.slice_in_dim(shard, length - width, length, axis=dim)
        leading = lax.slice_in_dim(shard, 0, width, axis=dim)
        before = lax.ppermute(last, axis, up)
        after = lax.ppermute(leading, axis, down)
        shard = jnp.concatenate([before, shard, after], axis=dim)
    return shard


def body(volume, kernel, grad_out):
    size_x, size_y, size_z, own_in = volume.shape
    total_out = kernel.shape[2]
    cells = size_x * size_y * size_z
    rim = padded_2(volume, (("sx", 0), ("sy", 1)), 1)
    padded = jnp.pad(rim, ((0, 0), (0, 0), (1, 1), (0, 0)))
    offsets = [(index // 9, index // 3 % 3, index % 3) for index in range(27)]
    partial_out = jnp.zeros((cells, total_out), jnp.float32)
    for index in range(27):
        a, b, e = offsets[index]
        window = padded[a : a + size_x, b : b + size_y, e : e + size_z].reshape(cells, own_in)
        partial_out = partial_out + jnp.dot(
            window, kernel[index], preferred_element_type=jnp.float32
        )
    partial_out = partial_out.reshape(size_x, size_y, size_z, total_out)
    out = lax.psum_scatter(partial_out, "chan", scatter_dimension=3, tiled=True).astype(
        jnp.bfloat16
    )
    grad_full = lax.all_gather(grad_out, "chan", axis=3, tiled=True)
    grad_rimmed = padded_2(grad_full, (("sx", 0), ("sy", 1)), 1)
    grad_padded = jnp.pad(grad_rimmed, ((0, 0), (0, 0), (1, 1), (0, 0)))
    flat_grad = grad_full.reshape(cells, total_out)
    back = jnp.zeros((cells, own_in), jnp.float32)
    kernel_terms = []
    for index in range(27):
        a, b, e = offsets[index]
        window = grad_padded[
            2 - a : 2 - a + size_x, 2 - b : 2 - b + size_y, 2 - e : 2 - e + size_z
        ].reshape(cells, total_out)
        back = back + lax.dot_general(
            window, kernel[index], (((1,), (1,)), ((), ())), preferred_element_type=jnp.float32
        )
        in_window = padded[a : a + size_x, b : b + size_y, e : e + size_z].reshape(cells, own_in)
        kernel_terms.append(
            lax.dot_general(
                in_window, flat_grad, (((0,), (0,)), ((), ())), preferred_element_type=jnp.float32
            )
        )
    grad_input = back.reshape(size_x, size_y, size_z, own_in).astype(jnp.bfloat16)
    local_kernel = jnp.stack(kernel_terms)
    summed = lax.psum(local_kernel, ("sx", "sy"))
    all_cells = cells * lax.axis_size("sx") * lax.axis_size("sy")
    grad_kernel = summed / jnp.float32(math.sqrt(all_cells))
    return (out, grad_input, grad_kernel)


MESH = pl.DeviceIdType.MESH
F32 = jnp.float32
BF16 = jnp.bfloat16


def fused_kernel(
    in_ref, w_ref, out_ref, gi_ref, gk_ref,
    blocks, gpad, v3, vt, part, from_near, from_far, side_block, side_rows,
    z_send, z_recv, p_send, p_recv, r_send, r_recv, k_send, k_recv, s_send, s_recv,
    *, scale,
):
    chans, count_s, count_h = lax.axis_size("chan"), lax.axis_size("sx"), lax.axis_size("sy")
    c, s, h = lax.axis_index("chan"), lax.axis_index("sx"), lax.axis_index("sy")
    rows_y, size_z, ch = in_ref.shape[1:]
    half = rows_y // 2
    cells = half * size_z
    total = w_ref.shape[2]
    wide = 3 * ch
    core, far_s, far_h = s + 1 - 2 * (s % 2), (s + 2) % 4, 1 - h
    others = (c + 1 - 2 * (c % 2), (c + 2) % 4, 3 - c)
    side = 3 - s
    to_x, to_y, to_core = {"sx": far_s}, {"sy": far_h}, {"sx": core}
    sent = []

    def remote(src, dst, send, recv, where):
        return pltpu.make_async_remote_copy(
            src_ref=src, dst_ref=dst, send_sem=send, recv_sem=recv,
            device_id=where, device_id_type=MESH,
        )

    def push(src, send, recv, where, dst=None):
        copy = remote(src, src if dst is None else dst, send, recv, where)
        copy.start()
        sent.append(copy)

    def arrived(ref, send, recv, where):
        remote(ref, ref, send, recv, where).wait_recv()

    barrier = pltpu.get_barrier_semaphore()
    to_side, to_side_row = {"sx": side}, {"sx": side, "sy": far_h}
    to_core_row = {"sx": core, "sy": far_h}
    partners = [{"chan": d} for d in others[:2]] + [to_x, to_y, to_core]
    partners += [to_side, to_side_row, to_core_row]
    for where in partners:
        pl.semaphore_signal(barrier, inc=1, device_id=where, device_id_type=MESH)

    zero_row = jnp.zeros((2, size_z, total // 2), BF16)
    last_x, last_y = gpad.shape[1] - 1, gpad.shape[2] - 1

    @pl.loop(0, last_y + 1)
    def _(y):
        for x in (0, last_x):
            gpad[:, x, y] = zero_row

    for x in range(1, last_x):
        for y in (0, last_y):
            gpad[:, x, y] = zero_row
    v3[...] = jnp.zeros(v3.shape, BF16)

    for k, index in enumerate((chans, c)):
        blocks[index, s, h, :, :, :ch] = in_ref[k, :half]
        blocks[index, s, h, :, :, ch:] = in_ref[k, half:]

    pl.semaphore_wait(barrier, len(partners))

    def offer(k, index):
        own = blocks.at[index, s, h]
        push(own, p_send.at[k, 0], p_recv.at[k, 0], to_x)
        push(own, p_send.at[k, 1], p_recv.at[k, 1], to_y)
        push(own, p_send.at[k, 2], p_recv.at[k, 2], to_core)

    def relay(k, index):
        from_x, from_y = blocks.at[index, far_s, h], blocks.at[index, s, far_h]
        cut = half // 2
        arrived(from_x, p_send.at[k, 0], p_recv.at[k, 0], to_x)
        push(from_x.at[:cut], p_send.at[k, 3], p_recv.at[k, 3], to_y)
        push(from_x, p_send.at[k, 5], p_recv.at[k, 5], to_core)
        arrived(from_y, p_send.at[k, 1], p_recv.at[k, 1], to_y)
        push(from_y.at[cut:], p_send.at[k, 4], p_recv.at[k, 4], to_x)
        push(from_y, p_send.at[k, 6], p_recv.at[k, 6], to_core)

    def corner(k, index):
        diag = blocks.at[index, far_s, far_h]
        cut = half // 2
        arrived(diag.at[:cut], p_send.at[k, 3], p_recv.at[k, 3], to_y)
        arrived(diag.at[cut:], p_send.at[k, 4], p_recv.at[k, 4], to_x)
        push(diag, p_send.at[k, 7], p_recv.at[k, 7], to_core)

    def near_core(k, index):
        arrived(blocks.at[index, core, h], p_send.at[k, 2], p_recv.at[k, 2], to_core)

    def far_core(k, index):
        arrived(blocks.at[index, side, h], p_send.at[k, 5], p_recv.at[k, 5], to_core)
        arrived(blocks.at[index, core, far_h], p_send.at[k, 6], p_recv.at[k, 6], to_core)
        arrived(blocks.at[index, side, far_h], p_send.at[k, 7], p_recv.at[k, 7], to_core)

    def from_chan(j):
        index = others[j]
        arrived(blocks.at[index, s, h], z_send.at[j], z_recv.at[j], {"chan": index})
        offer(j + 2, index)

    own, edge = blocks.at[chans, s, h], blocks.at[chans, s, h, (half - 1) * (1 - h)]
    inner = (s >= 1) & (s <= count_s - 2)
    side_copies = [
        remote(own, side_block, s_send.at[0], s_recv.at[0], to_side),
        remote(edge, side_rows.at[1], s_send.at[1], s_recv.at[1], to_side_row),
    ]
    core_row = remote(edge, side_rows.at[0], s_send.at[2], s_recv.at[2], to_core_row)
    core_row.start()

    @pl.when(inner)
    def _():
        for copy in side_copies:
            copy.start()

    offer(0, chans)
    for j, d in enumerate(others[:2]):
        push(blocks.at[c, s, h], z_send.at[j], z_recv.at[j], {"chan": d})
    offer(1, c)

    def shifted(block):
        wide_block = block.astype(F32)
        row = lax.broadcasted_iota(jnp.int32, block.shape, 0) % size_z
        before = jnp.where(row == 0, 0.0, pltpu.roll(wide_block, 1, 0))
        after = jnp.where(row == size_z - 1, 0.0, pltpu.roll(wide_block, block.shape[0] - 1, 0))
        return before.astype(BF16), block, after.astype(BF16)

    def spread(dx, block):
        parts = shifted(block.reshape(cells, 2 * ch))
        parts = [moved.reshape(half, size_z, 2 * ch) for moved in parts]
        for k in range(2):
            v3[dx, 1 + k * half : 1 + (k + 1) * half] = jnp.concatenate(
                [moved[:, :, k * ch : (k + 1) * ch] for moved in parts], axis=-1
            )

    def spread_edge(dx, rows):
        parts = shifted(rows)
        for at_h, lanes, row_at in ((0, slice(0, ch), rows_y + 1), (1, slice(ch, 2 * ch), 0)):
            @pl.when(h == at_h)
            def _():
                v3[dx, row_at] = jnp.concatenate([moved[:, lanes] for moved in parts], axis=-1)

    spread(1, own[...])
    relay(0, chans)
    near_core(0, chans)
    core_row.wait()
    dx_core, dx_side = 2 - 2 * (s % 2), 2 * (s % 2)
    spread(dx_core, blocks[chans, core, h])
    spread_edge(1, blocks[chans, s, far_h, (half - 1) * h])
    spread_edge(dx_core, side_rows[0])

    @pl.when(inner)
    def _():
        for copy in side_copies:
            copy.wait()
        spread(dx_side, side_block[...])
        spread_edge(dx_side, side_rows[1])

    from_chan(0)
    from_chan(1)
    push(blocks.at[others[1], s, h], z_send.at[2], z_recv.at[2], {"chan": others[0]})

    for t in range(2):
        acc = jnp.zeros((cells, total), F32)
        for a in range(3):
            for b in range(3):
                window = v3[a, t * half + b : t * half + b + half].reshape(cells, wide)
                acc = acc + jnp.dot(window, w_ref[3 * a + b], preferred_element_type=F32)
        for d in range(chans):
            for k in range(2):
                part[d, t, :, k * ch : (k + 1) * ch] = (
                    acc[k * cells // 2 : (k + 1) * cells // 2, d * ch : (d + 1) * ch]
                )
        for k, d in enumerate((others[0], others[2])):
            push(
                part.at[d, t], r_send.at[t, k], r_recv.at[t, k], {"chan": others[0]},
                dst=from_near.at[k, t],
            )

    def pair_sum(t):
        for k in (1, 0):
            arrived(from_near.at[k, t], r_send.at[t, k], r_recv.at[t, k], {"chan": others[0]})
        part[others[1], t] = part[others[1], t] + from_near[1, t]
        push(
            part.at[others[1], t], r_send.at[t, 2], r_recv.at[t, 2], {"chan": others[1]},
            dst=from_far.at[t],
        )

    relay(1, c)
    corner(0, chans)
    relay(2, others[0])
    corner(1, c)
    far_core(0, chans)

    def turn(n):
        x, hy = n // count_h, n % count_h
        for e, moved in enumerate(shifted(blocks[chans, x, hy].reshape(cells, 2 * ch))):
            turned = moved.T
            for k in range(2):
                at = pl.multiple_of((hy * 2 + k) * cells, cells)
                vt[x, e * ch : (e + 1) * ch, pl.ds(at, cells)] = turned[k * ch : (k + 1) * ch]

    turns = count_s * count_h
    pl.loop(0, turns // 4)(turn)
    from_chan(2)
    relay(3, others[1])
    corner(2, others[0])
    pl.loop(turns // 4, turns // 2)(turn)
    pair_sum(0)
    pl.loop(turns // 2, 3 * turns // 4)(turn)
    relay(4, others[2])
    pair_sum(1)
    pl.loop(3 * turns // 4, turns)(turn)
    corner(3, others[1])
    corner(4, others[2])

    def fill(pair):
        @pl.loop(0, count_s * count_h)
        def _(n):
            x, hy = n // count_h, n % count_h
            one, two = blocks[2 * pair, x, hy], blocks[2 * pair + 1, x, hy]
            for k in range(2):
                lanes = slice(k * ch, (k + 1) * ch)
                gpad[pair, x + 1, pl.ds(1 + hy * rows_y + k * half, half)] = jnp.concatenate(
                    [one[:, :, lanes], two[:, :, lanes]], axis=-1
                )

    everything = list(enumerate((c,) + others, 1))
    for now, pair in ((everything[:2], c // 2), (everything[2:], 1 - c // 2)):
        for k, index in now:
            near_core(k, index)
            far_core(k, index)
        fill(pair)

    def cotangent(x, start, rows):
        return jnp.concatenate(
            [gpad[p, x, pl.ds(start, rows)].reshape(rows * size_z, total // 2) for p in range(2)],
            axis=-1,
        )

    core_at = s % 2
    all_y = rows_y * count_h
    top = wide // 2

    def weight_gradient(step, index, terms, at, rows):
        acc = jnp.zeros((rows, total), F32)
        for x_in, x_out, start in terms:
            acc = acc + jnp.dot(
                vt[x_in, pl.ds(at, rows), :], cotangent(x_out, start, all_y),
                preferred_element_type=F32,
            )
        gk_ref[index, pl.ds(at, rows)] = acc / scale
        push(gk_ref.at[index, pl.ds(at, rows)], k_send.at[step], k_recv.at[step], to_core)

    for b in range(3):
        weight_gradient(
            b, 6 * core_at + b,
            [(x + core_at, x + 2 - core_at, 2 - b) for x in range(count_s - 1)], 0, wide,
        )
    weight_gradient(
        3, 3 + 2 * core_at, [(x, x + 1, 2 - 2 * core_at) for x in range(count_s)], 0, wide
    )
    weight_gradient(
        4, 4, [(x, x + 1, 1) for x in range(count_s)], pl.multiple_of(core_at * top, top), top
    )

    row_out = lax.broadcasted_iota(jnp.int32, (2 * cells, ch), 0) % size_z
    acc = jnp.zeros((2 * cells, wide), F32)
    for a in range(3):
        for b in range(3):
            acc = acc + lax.dot_general(
                cotangent(s + 2 - a, h * rows_y + 2 - b, rows_y), w_ref[3 * a + b],
                (((1,), (1,)), ((), ())), preferred_element_type=F32,
            )
    first, middle, final = acc[:, :ch], acc[:, ch : 2 * ch], acc[:, 2 * ch :]
    later = jnp.where(row_out == size_z - 1, 0.0, pltpu.roll(first, 2 * cells - 1, 0))
    sooner = jnp.where(row_out == 0, 0.0, pltpu.roll(final, 1, 0))
    gi_ref[0] = (later + middle + sooner).astype(BF16).reshape(rows_y, size_z, ch)

    for t in range(2):
        arrived(from_far.at[t], r_send.at[t, 2], r_recv.at[t, 2], {"chan": others[1]})
        summed = part[c, t] + from_near[0, t] + from_far[t]
        narrow = summed.astype(BF16).reshape(half // 2, size_z, 2 * ch)
        for k in range(2):
            at = t * half + k * (half // 2)
            out_ref[0, at : at + half // 2] = narrow[:, :, k * ch : (k + 1) * ch]

    for b in range(3):
        arrived(gk_ref.at[6 * (1 - core_at) + b], k_send.at[b], k_recv.at[b], to_core)
    arrived(gk_ref.at[5 - 2 * core_at], k_send.at[3], k_recv.at[3], to_core)
    below = pl.multiple_of((1 - core_at) * top, top)
    arrived(gk_ref.at[4, pl.ds(below, top)], k_send.at[4], k_recv.at[4], to_core)
    for copy in sent:
        copy.wait_send()


def fused_body(volume, kernel, grad_out):
    chans, count_s, count_h = lax.axis_size("chan"), lax.axis_size("sx"), lax.axis_size("sy")
    _, rows_y, size_z, ch = volume.shape
    total = kernel.shape[2]
    half, wide = rows_y // 2, 3 * ch
    cells = half * size_z
    all_y = rows_y * count_h
    scale = math.sqrt(count_s * all_y * size_z)
    weights = kernel.reshape(9, wide, total)
    vmem = pl.BlockSpec(memory_space=pltpu.VMEM)
    dma = pltpu.SemaphoreType.DMA
    out, gi, gk = pl.pallas_call(
        functools.partial(fused_kernel, scale=scale),
        out_shape=(
            jax.ShapeDtypeStruct(volume.shape, BF16),
            jax.ShapeDtypeStruct(volume.shape, BF16),
            jax.ShapeDtypeStruct(weights.shape, F32),
        ),
        in_specs=[vmem] * 2,
        out_specs=(vmem,) * 3,
        scratch_shapes=[
            pltpu.VMEM((chans + 1, count_s, count_h, half, size_z, 2 * ch), BF16),
            pltpu.VMEM((2, count_s + 2, all_y + 2, size_z, total // 2), BF16),
            pltpu.VMEM((3, rows_y + 2, size_z, wide), BF16),
            pltpu.VMEM((count_s, wide, 2 * count_h * cells), BF16),
            pltpu.VMEM((chans, 2, cells // 2, 2 * ch), F32),
            pltpu.VMEM((2, 2, cells // 2, 2 * ch), F32),
            pltpu.VMEM((2, cells // 2, 2 * ch), F32),
            pltpu.VMEM((half, size_z, 2 * ch), BF16),
            pltpu.VMEM((2, size_z, 2 * ch), BF16),
            dma((3,)), dma((3,)),
            dma((chans + 1, 8)), dma((chans + 1, 8)),
            dma((2, 3)), dma((2, 3)),
            dma((5,)), dma((5,)),
            dma((3,)), dma((3,)),
        ],
        compiler_params=pltpu.CompilerParams(
            collective_id=0, has_side_effects=True, vmem_limit_bytes=50 * 2**20
        ),
    )(jnp.concatenate([volume, grad_out]), weights)
    return out, gi, gk.reshape(kernel.shape)


def solution(mesh):
    small = (mesh.shape["chan"], mesh.shape["sx"], mesh.shape["sy"]) == (4, 4, 2)
    return jax.shard_map(
        fused_body if small else body,
        mesh=mesh,
        in_specs=(P("sx", "sy", None, "chan"), P(None, "chan", None), P("sx", "sy", None, "chan")),
        out_specs=(P("sx", "sy", None, "chan"), P("sx", "sy", None, "chan"), P(None, "chan", None)),
        check_vma=False,
    )
```

```python
import functools
import math

import jax
import jax.numpy as jnp
from jax import lax
from jax.experimental import pallas as pl
from jax.experimental.pallas import tpu as pltpu
from jax.sharding import PartitionSpec as P


def padded_2(shard, sides, width):
    for axis, dim in sides:
        count, length = (lax.axis_size(axis), shard.shape[dim])
        up = [(i, (i + 1) % count) for i in range(count - 1)]
        down = [(j, i) for i, j in up]
        last = lax.slice_in_dim(shard, length - width, length, axis=dim)
        leading = lax.slice_in_dim(shard, 0, width, axis=dim)
        before = lax.ppermute(last, axis, up)
        after = lax.ppermute(leading, axis, down)
        shard = jnp.concatenate([before, shard, after], axis=dim)
    return shard


def body(volume, kernel, grad_out):
    size_x, size_y, size_z, own_in = volume.shape
    total_out = kernel.shape[2]
    cells = size_x * size_y * size_z
    rim = padded_2(volume, (("sx", 0), ("sy", 1)), 1)
    padded = jnp.pad(rim, ((0, 0), (0, 0), (1, 1), (0, 0)))
    offsets = [(index // 9, index // 3 % 3, index % 3) for index in range(27)]
    partial_out = jnp.zeros((cells, total_out), jnp.float32)
    for index in range(27):
        a, b, e = offsets[index]
        window = padded[a : a + size_x, b : b + size_y, e : e + size_z].reshape(cells, own_in)
        partial_out = partial_out + jnp.dot(
            window, kernel[index], preferred_element_type=jnp.float32
        )
    partial_out = partial_out.reshape(size_x, size_y, size_z, total_out)
    out = lax.psum_scatter(partial_out, "chan", scatter_dimension=3, tiled=True).astype(
        jnp.bfloat16
    )
    grad_full = lax.all_gather(grad_out, "chan", axis=3, tiled=True)
    grad_rimmed = padded_2(grad_full, (("sx", 0), ("sy", 1)), 1)
    grad_padded = jnp.pad(grad_rimmed, ((0, 0), (0, 0), (1, 1), (0, 0)))
    flat_grad = grad_full.reshape(cells, total_out)
    back = jnp.zeros((cells, own_in), jnp.float32)
    kernel_terms = []
    for index in range(27):
        a, b, e = offsets[index]
        window = grad_padded[
            2 - a : 2 - a + size_x, 2 - b : 2 - b + size_y, 2 - e : 2 - e + size_z
        ].reshape(cells, total_out)
        back = back + lax.dot_general(
            window, kernel[index], (((1,), (1,)), ((), ())), preferred_element_type=jnp.float32
        )
        in_window = padded[a : a + size_x, b : b + size_y, e : e + size_z].reshape(cells, own_in)
        kernel_terms.append(
            lax.dot_general(
                in_window, flat_grad, (((0,), (0,)), ((), ())), preferred_element_type=jnp.float32
            )
        )
    grad_input = back.reshape(size_x, size_y, size_z, own_in).astype(jnp.bfloat16)
    local_kernel = jnp.stack(kernel_terms)
    summed = lax.psum(local_kernel, ("sx", "sy"))
    all_cells = cells * lax.axis_size("sx") * lax.axis_size("sy")
    grad_kernel = summed / jnp.float32(math.sqrt(all_cells))
    return (out, grad_input, grad_kernel)


MESH = pl.DeviceIdType.MESH
F32 = jnp.float32
BF16 = jnp.bfloat16


def fused_kernel(
    in_ref, w_ref, out_ref, gi_ref, gk_ref,
    blocks, gpad, v3, vt, part, from_near, from_far, side_block, side_rows,
    z_send, z_recv, p_send, p_recv, r_send, r_recv, k_send, k_recv, s_send, s_recv,
    *, scale,
):
    chans, count_s, count_h = lax.axis_size("chan"), lax.axis_size("sx"), lax.axis_size("sy")
    c, s, h = lax.axis_index("chan"), lax.axis_index("sx"), lax.axis_index("sy")
    rows_y, size_z, ch = in_ref.shape[1:]
    half = rows_y // 2
    cells = half * size_z
    total = w_ref.shape[2]
    wide = 3 * ch
    core, far_s, far_h = s + 1 - 2 * (s % 2), (s + 2) % 4, 1 - h
    others = (c + 1 - 2 * (c % 2), (c + 2) % 4, 3 - c)
    side = 3 - s
    to_x, to_y, to_core = {"sx": far_s}, {"sy": far_h}, {"sx": core}
    sent = []

    def remote(src, dst, send, recv, where):
        return pltpu.make_async_remote_copy(
            src_ref=src, dst_ref=dst, send_sem=send, recv_sem=recv,
            device_id=where, device_id_type=MESH,
        )

    def push(src, send, recv, where, dst=None):
        copy = remote(src, src if dst is None else dst, send, recv, where)
        copy.start()
        sent.append(copy)

    def arrived(ref, send, recv, where):
        remote(ref, ref, send, recv, where).wait_recv()

    barrier = pltpu.get_barrier_semaphore()
    to_side, to_side_row = {"sx": side}, {"sx": side, "sy": far_h}
    to_core_row = {"sx": core, "sy": far_h}
    partners = [{"chan": d} for d in others[:2]] + [to_x, to_y, to_core]
    partners += [to_side, to_side_row, to_core_row]
    for where in partners:
        pl.semaphore_signal(barrier, inc=1, device_id=where, device_id_type=MESH)

    zero_row = jnp.zeros((2, size_z, total // 2), BF16)
    last_x, last_y = gpad.shape[1] - 1, gpad.shape[2] - 1

    @pl.loop(0, last_y + 1)
    def _(y):
        for x in (0, last_x):
            gpad[:, x, y] = zero_row

    for x in range(1, last_x):
        for y in (0, last_y):
            gpad[:, x, y] = zero_row
    v3[...] = jnp.zeros(v3.shape, BF16)

    for k, index in enumerate((chans, c)):
        blocks[index, s, h, :, :, :ch] = in_ref[k, :half]
        blocks[index, s, h, :, :, ch:] = in_ref[k, half:]

    pl.semaphore_wait(barrier, len(partners))

    def offer(k, index):
        own = blocks.at[index, s, h]
        push(own, p_send.at[k, 0], p_recv.at[k, 0], to_x)
        push(own, p_send.at[k, 1], p_recv.at[k, 1], to_y)
        push(own, p_send.at[k, 2], p_recv.at[k, 2], to_core)

    def relay(k, index):
        from_x, from_y = blocks.at[index, far_s, h], blocks.at[index, s, far_h]
        cut = half // 2
        arrived(from_x, p_send.at[k, 0], p_recv.at[k, 0], to_x)
        push(from_x.at[:cut], p_send.at[k, 3], p_recv.at[k, 3], to_y)
        push(from_x, p_send.at[k, 5], p_recv.at[k, 5], to_core)
        arrived(from_y, p_send.at[k, 1], p_recv.at[k, 1], to_y)
        push(from_y.at[cut:], p_send.at[k, 4], p_recv.at[k, 4], to_x)
        push(from_y, p_send.at[k, 6], p_recv.at[k, 6], to_core)

    def corner(k, index):
        diag = blocks.at[index, far_s, far_h]
        cut = half // 2
        arrived(diag.at[:cut], p_send.at[k, 3], p_recv.at[k, 3], to_y)
        arrived(diag.at[cut:], p_send.at[k, 4], p_recv.at[k, 4], to_x)
        push(diag, p_send.at[k, 7], p_recv.at[k, 7], to_core)

    def near_core(k, index):
        arrived(blocks.at[index, core, h], p_send.at[k, 2], p_recv.at[k, 2], to_core)

    def far_core(k, index):
        arrived(blocks.at[index, side, h], p_send.at[k, 5], p_recv.at[k, 5], to_core)
        arrived(blocks.at[index, core, far_h], p_send.at[k, 6], p_recv.at[k, 6], to_core)
        arrived(blocks.at[index, side, far_h], p_send.at[k, 7], p_recv.at[k, 7], to_core)

    def from_chan(j):
        index = others[j]
        arrived(blocks.at[index, s, h], z_send.at[j], z_recv.at[j], {"chan": index})
        offer(j + 2, index)

    own, edge = blocks.at[chans, s, h], blocks.at[chans, s, h, (half - 1) * (1 - h)]
    inner = (s >= 1) & (s <= count_s - 2)
    side_copies = [
        remote(own, side_block, s_send.at[0], s_recv.at[0], to_side),
        remote(edge, side_rows.at[1], s_send.at[1], s_recv.at[1], to_side_row),
    ]
    core_row = remote(edge, side_rows.at[0], s_send.at[2], s_recv.at[2], to_core_row)
    core_row.start()

    @pl.when(inner)
    def _():
        for copy in side_copies:
            copy.start()

    offer(0, chans)
    for j, d in enumerate(others[:2]):
        push(blocks.at[c, s, h], z_send.at[j], z_recv.at[j], {"chan": d})
    offer(1, c)

    def shifted(block):
        wide_block = block.astype(F32)
        row = lax.broadcasted_iota(jnp.int32, block.shape, 0) % size_z
        before = jnp.where(row == 0, 0.0, pltpu.roll(wide_block, 1, 0))
        after = jnp.where(row == size_z - 1, 0.0, pltpu.roll(wide_block, block.shape[0] - 1, 0))
        return before.astype(BF16), block, after.astype(BF16)

    def spread(dx, block):
        parts = shifted(block.reshape(cells, 2 * ch))
        parts = [moved.reshape(half, size_z, 2 * ch) for moved in parts]
        for k in range(2):
            v3[dx, 1 + k * half : 1 + (k + 1) * half] = jnp.concatenate(
                [moved[:, :, k * ch : (k + 1) * ch] for moved in parts], axis=-1
            )

    def spread_edge(dx, rows):
        parts = shifted(rows)
        for at_h, lanes, row_at in ((0, slice(0, ch), rows_y + 1), (1, slice(ch, 2 * ch), 0)):
            @pl.when(h == at_h)
            def _():
                v3[dx, row_at] = jnp.concatenate([moved[:, lanes] for moved in parts], axis=-1)

    spread(1, own[...])
    relay(0, chans)
    near_core(0, chans)
    core_row.wait()
    dx_core, dx_side = 2 - 2 * (s % 2), 2 * (s % 2)
    spread(dx_core, blocks[chans, core, h])
    spread_edge(1, blocks[chans, s, far_h, (half - 1) * h])
    spread_edge(dx_core, side_rows[0])

    @pl.when(inner)
    def _():
        for copy in side_copies:
            copy.wait()
        spread(dx_side, side_block[...])
        spread_edge(dx_side, side_rows[1])

    from_chan(0)
    from_chan(1)
    push(blocks.at[others[1], s, h], z_send.at[2], z_recv.at[2], {"chan": others[0]})

    for t in range(2):
        acc = jnp.zeros((cells, total), F32)
        for a in range(3):
            for b in range(3):
                window = v3[a, t * half + b : t * half + b + half].reshape(cells, wide)
                acc = acc + jnp.dot(window, w_ref[3 * a + b], preferred_element_type=F32)
        for d in range(chans):
            for k in range(2):
                part[d, t, :, k * ch : (k + 1) * ch] = (
                    acc[k * cells // 2 : (k + 1) * cells // 2, d * ch : (d + 1) * ch]
                )
        for k, d in enumerate((others[0], others[2])):
            push(
                part.at[d, t], r_send.at[t, k], r_recv.at[t, k], {"chan": others[0]},
                dst=from_near.at[k, t],
            )

    def pair_sum(t):
        for k in (1, 0):
            arrived(from_near.at[k, t], r_send.at[t, k], r_recv.at[t, k], {"chan": others[0]})
        part[others[1], t] = part[others[1], t] + from_near[1, t]
        push(
            part.at[others[1], t], r_send.at[t, 2], r_recv.at[t, 2], {"chan": others[1]},
            dst=from_far.at[t],
        )

    relay(1, c)
    corner(0, chans)
    relay(2, others[0])
    corner(1, c)
    far_core(0, chans)

    def turn(n):
        x, hy = n // count_h, n % count_h
        for e, moved in enumerate(shifted(blocks[chans, x, hy].reshape(cells, 2 * ch))):
            turned = moved.T
            for k in range(2):
                at = pl.multiple_of((hy * 2 + k) * cells, cells)
                vt[x, e * ch : (e + 1) * ch, pl.ds(at, cells)] = turned[k * ch : (k + 1) * ch]

    turns = count_s * count_h
    def fill(pair):
        @pl.loop(0, count_s * count_h)
        def _(n):
            x, hy = n // count_h, n % count_h
            one, two = blocks[2 * pair, x, hy], blocks[2 * pair + 1, x, hy]
            for k in range(2):
                lanes = slice(k * ch, (k + 1) * ch)
                gpad[pair, x + 1, pl.ds(1 + hy * rows_y + k * half, half)] = jnp.concatenate(
                    [one[:, :, lanes], two[:, :, lanes]], axis=-1
                )

    def cotangent(x, start, rows):
        return jnp.concatenate(
            [gpad[p, x, pl.ds(start, rows)].reshape(rows * size_z, total // 2) for p in range(2)],
            axis=-1,
        )

    core_at = s % 2
    all_y = rows_y * count_h
    top = wide // 2

    def weight_gradient(step, pair, index, terms, at, rows):
        acc = jnp.zeros((rows, total // 2), F32)
        for x_in, x_out, start in terms:
            window = gpad[pair, x_out, pl.ds(start, all_y)].reshape(all_y * size_z, total // 2)
            acc = acc + jnp.dot(
                vt[x_in, pl.ds(at, rows), :], window, preferred_element_type=F32
            )
        gk_ref[pair, index, pl.ds(at, rows)] = acc / scale
        push(
            gk_ref.at[pair, index, pl.ds(at, rows)],
            k_send.at[step], k_recv.at[step], to_core,
        )

    def step_of(pair, first, step):
        if step < 3:
            weight_gradient(
                first + step, pair, 6 * core_at + step,
                [(x + core_at, x + 2 - core_at, 2 - step) for x in range(count_s - 1)], 0, wide,
            )
        elif step == 3:
            weight_gradient(
                first + step, pair, 3 + 2 * core_at,
                [(x, x + 1, 2 - 2 * core_at) for x in range(count_s)], 0, wide,
            )
        else:
            weight_gradient(
                first + step, pair, 4, [(x, x + 1, 1) for x in range(count_s)],
                pl.multiple_of(core_at * top, top), top,
            )

    pl.loop(0, turns // 2)(turn)
    from_chan(2)
    relay(3, others[1])
    corner(2, others[0])
    pl.loop(turns // 2, turns)(turn)

    mine, other = c // 2, 1 - c // 2
    for k, index in ((1, c), (2, others[0])):
        near_core(k, index)
        far_core(k, index)
    fill(mine)
    pair_sum(0)
    step_of(mine, 0, 0)
    step_of(mine, 0, 1)
    relay(4, others[2])
    step_of(mine, 0, 2)
    pair_sum(1)
    corner(3, others[1])
    step_of(mine, 0, 3)
    corner(4, others[2])
    step_of(mine, 0, 4)
    for k, index in ((3, others[1]), (4, others[2])):
        near_core(k, index)
        far_core(k, index)
    fill(other)
    for step in range(5):
        step_of(other, 5, step)

    row_out = lax.broadcasted_iota(jnp.int32, (2 * cells, ch), 0) % size_z
    acc = jnp.zeros((2 * cells, wide), F32)
    for a in range(3):
        for b in range(3):
            acc = acc + lax.dot_general(
                cotangent(s + 2 - a, h * rows_y + 2 - b, rows_y), w_ref[3 * a + b],
                (((1,), (1,)), ((), ())), preferred_element_type=F32,
            )
    first, middle, final = acc[:, :ch], acc[:, ch : 2 * ch], acc[:, 2 * ch :]
    later = jnp.where(row_out == size_z - 1, 0.0, pltpu.roll(first, 2 * cells - 1, 0))
    sooner = jnp.where(row_out == 0, 0.0, pltpu.roll(final, 1, 0))
    gi_ref[0] = (later + middle + sooner).astype(BF16).reshape(rows_y, size_z, ch)

    for t in range(2):
        arrived(from_far.at[t], r_send.at[t, 2], r_recv.at[t, 2], {"chan": others[1]})
        summed = part[c, t] + from_near[0, t] + from_far[t]
        narrow = summed.astype(BF16).reshape(half // 2, size_z, 2 * ch)
        for k in range(2):
            at = t * half + k * (half // 2)
            out_ref[0, at : at + half // 2] = narrow[:, :, k * ch : (k + 1) * ch]

    below = pl.multiple_of((1 - core_at) * top, top)
    for first, pair in ((0, mine), (5, other)):
        theirs = [gk_ref.at[pair, 6 * (1 - core_at) + b] for b in range(3)]
        theirs += [gk_ref.at[pair, 5 - 2 * core_at], gk_ref.at[pair, 4, pl.ds(below, top)]]
        for step, ref in enumerate(theirs):
            arrived(ref, k_send.at[first + step], k_recv.at[first + step], to_core)
    for copy in sent:
        copy.wait_send()


def store_kernel(out_in, gi_in, gk_in, out_ref, gi_ref, gk_ref, sem):
    lanes = gk_in.shape[3]
    copies = [
        pltpu.make_async_copy(gk_in.at[p], gk_ref.at[:, :, pl.ds(p * lanes, lanes)], sem.at[p])
        for p in range(2)
    ]
    copies.append(pltpu.make_async_copy(out_in, out_ref, sem.at[2]))
    copies.append(pltpu.make_async_copy(gi_in, gi_ref, sem.at[3]))
    for copy in copies:
        copy.start()
    for copy in copies:
        copy.wait()


def fused_body(volume, kernel, grad_out):
    chans, count_s, count_h = lax.axis_size("chan"), lax.axis_size("sx"), lax.axis_size("sy")
    _, rows_y, size_z, ch = volume.shape
    total = kernel.shape[2]
    half, wide = rows_y // 2, 3 * ch
    cells = half * size_z
    all_y = rows_y * count_h
    scale = math.sqrt(count_s * all_y * size_z)
    weights = kernel.reshape(9, wide, total)
    vmem = pl.BlockSpec(memory_space=pltpu.VMEM)
    dma = pltpu.SemaphoreType.DMA
    out, gi, gk = pl.pallas_call(
        functools.partial(fused_kernel, scale=scale),
        out_shape=(
            jax.ShapeDtypeStruct(volume.shape, BF16),
            jax.ShapeDtypeStruct(volume.shape, BF16),
            jax.ShapeDtypeStruct((2, 9, wide, total // 2), F32),
        ),
        in_specs=[vmem] * 2,
        out_specs=(vmem,) * 3,
        scratch_shapes=[
            pltpu.VMEM((chans + 1, count_s, count_h, half, size_z, 2 * ch), BF16),
            pltpu.VMEM((2, count_s + 2, all_y + 2, size_z, total // 2), BF16),
            pltpu.VMEM((3, rows_y + 2, size_z, wide), BF16),
            pltpu.VMEM((count_s, wide, 2 * count_h * cells), BF16),
            pltpu.VMEM((chans, 2, cells // 2, 2 * ch), F32),
            pltpu.VMEM((2, 2, cells // 2, 2 * ch), F32),
            pltpu.VMEM((2, cells // 2, 2 * ch), F32),
            pltpu.VMEM((half, size_z, 2 * ch), BF16),
            pltpu.VMEM((2, size_z, 2 * ch), BF16),
            dma((3,)), dma((3,)),
            dma((chans + 1, 8)), dma((chans + 1, 8)),
            dma((2, 3)), dma((2, 3)),
            dma((10,)), dma((10,)),
            dma((3,)), dma((3,)),
        ],
        compiler_params=pltpu.CompilerParams(
            collective_id=0, has_side_effects=True, vmem_limit_bytes=50 * 2**20
        ),
    )(jnp.concatenate([volume, grad_out]), weights)
    out, gi, gk = pl.pallas_call(
        store_kernel,
        out_shape=(
            jax.ShapeDtypeStruct(volume.shape, BF16),
            jax.ShapeDtypeStruct(volume.shape, BF16),
            jax.ShapeDtypeStruct(weights.shape, F32),
        ),
        in_specs=[vmem] * 3,
        out_specs=(pl.BlockSpec(memory_space=pltpu.MemorySpace.HBM),) * 3,
        scratch_shapes=[dma((4,))],
    )(out, gi, gk)
    return out, gi, gk.reshape(kernel.shape)


def solution(mesh):
    small = (mesh.shape["chan"], mesh.shape["sx"], mesh.shape["sy"]) == (4, 4, 2)
    return jax.shard_map(
        fused_body if small else body,
        mesh=mesh,
        in_specs=(P("sx", "sy", None, "chan"), P(None, "chan", None), P("sx", "sy", None, "chan")),
        out_specs=(P("sx", "sy", None, "chan"), P("sx", "sy", None, "chan"), P(None, "chan", None)),
        check_vma=False,
    )
```

```python
import functools
import math

import jax
import jax.numpy as jnp
from jax import lax
from jax.experimental import pallas as pl
from jax.experimental.pallas import tpu as pltpu
from jax.sharding import PartitionSpec as P


def padded_2(shard, sides, width):
    for axis, dim in sides:
        count, length = (lax.axis_size(axis), shard.shape[dim])
        up = [(i, (i + 1) % count) for i in range(count - 1)]
        down = [(j, i) for i, j in up]
        last = lax.slice_in_dim(shard, length - width, length, axis=dim)
        leading = lax.slice_in_dim(shard, 0, width, axis=dim)
        before = lax.ppermute(last, axis, up)
        after = lax.ppermute(leading, axis, down)
        shard = jnp.concatenate([before, shard, after], axis=dim)
    return shard


def body(volume, kernel, grad_out):
    size_x, size_y, size_z, own_in = volume.shape
    total_out = kernel.shape[2]
    cells = size_x * size_y * size_z
    rim = padded_2(volume, (("sx", 0), ("sy", 1)), 1)
    padded = jnp.pad(rim, ((0, 0), (0, 0), (1, 1), (0, 0)))
    offsets = [(index // 9, index // 3 % 3, index % 3) for index in range(27)]
    partial_out = jnp.zeros((cells, total_out), jnp.float32)
    for index in range(27):
        a, b, e = offsets[index]
        window = padded[a : a + size_x, b : b + size_y, e : e + size_z].reshape(cells, own_in)
        partial_out = partial_out + jnp.dot(
            window, kernel[index], preferred_element_type=jnp.float32
        )
    partial_out = partial_out.reshape(size_x, size_y, size_z, total_out)
    out = lax.psum_scatter(partial_out, "chan", scatter_dimension=3, tiled=True).astype(
        jnp.bfloat16
    )
    grad_full = lax.all_gather(grad_out, "chan", axis=3, tiled=True)
    grad_rimmed = padded_2(grad_full, (("sx", 0), ("sy", 1)), 1)
    grad_padded = jnp.pad(grad_rimmed, ((0, 0), (0, 0), (1, 1), (0, 0)))
    flat_grad = grad_full.reshape(cells, total_out)
    back = jnp.zeros((cells, own_in), jnp.float32)
    kernel_terms = []
    for index in range(27):
        a, b, e = offsets[index]
        window = grad_padded[
            2 - a : 2 - a + size_x, 2 - b : 2 - b + size_y, 2 - e : 2 - e + size_z
        ].reshape(cells, total_out)
        back = back + lax.dot_general(
            window, kernel[index], (((1,), (1,)), ((), ())), preferred_element_type=jnp.float32
        )
        in_window = padded[a : a + size_x, b : b + size_y, e : e + size_z].reshape(cells, own_in)
        kernel_terms.append(
            lax.dot_general(
                in_window, flat_grad, (((0,), (0,)), ((), ())), preferred_element_type=jnp.float32
            )
        )
    grad_input = back.reshape(size_x, size_y, size_z, own_in).astype(jnp.bfloat16)
    local_kernel = jnp.stack(kernel_terms)
    summed = lax.psum(local_kernel, ("sx", "sy"))
    all_cells = cells * lax.axis_size("sx") * lax.axis_size("sy")
    grad_kernel = summed / jnp.float32(math.sqrt(all_cells))
    return (out, grad_input, grad_kernel)


MESH = pl.DeviceIdType.MESH
F32 = jnp.float32
BF16 = jnp.bfloat16


def fused_kernel(
    in_ref, w_ref, out_ref, gi_ref, gk_ref,
    blocks, gpad, v3, vt, part, from_near, from_far, side_block, side_rows, back,
    z_send, z_recv, p_send, p_recv, r_send, r_recv, k_send, k_recv, s_send, s_recv,
    *, scale,
):
    chans, count_s, count_h = lax.axis_size("chan"), lax.axis_size("sx"), lax.axis_size("sy")
    c, s, h = lax.axis_index("chan"), lax.axis_index("sx"), lax.axis_index("sy")
    rows_y, size_z, ch = in_ref.shape[1:]
    half = rows_y // 2
    cells = half * size_z
    total = w_ref.shape[2]
    wide = 3 * ch
    core, far_s, far_h = s + 1 - 2 * (s % 2), (s + 2) % 4, 1 - h
    others = (c + 1 - 2 * (c % 2), (c + 2) % 4, 3 - c)
    side = 3 - s
    to_x, to_y, to_core = {"sx": far_s}, {"sy": far_h}, {"sx": core}
    sent = []

    def remote(src, dst, send, recv, where):
        return pltpu.make_async_remote_copy(
            src_ref=src, dst_ref=dst, send_sem=send, recv_sem=recv,
            device_id=where, device_id_type=MESH,
        )

    def push(src, send, recv, where, dst=None):
        copy = remote(src, src if dst is None else dst, send, recv, where)
        copy.start()
        sent.append(copy)

    def arrived(ref, send, recv, where):
        remote(ref, ref, send, recv, where).wait_recv()

    barrier = pltpu.get_barrier_semaphore()
    to_side, to_side_row = {"sx": side}, {"sx": side, "sy": far_h}
    to_core_row = {"sx": core, "sy": far_h}
    partners = [{"chan": d} for d in others[:2]] + [to_x, to_y, to_core]
    partners += [to_side, to_side_row, to_core_row]
    for where in partners:
        pl.semaphore_signal(barrier, inc=1, device_id=where, device_id_type=MESH)

    zero_row = jnp.zeros((2, size_z, total // 2), BF16)
    last_x, last_y = gpad.shape[1] - 1, gpad.shape[2] - 1

    @pl.loop(0, last_y + 1)
    def _(y):
        for x in (0, last_x):
            gpad[:, x, y] = zero_row

    for x in range(1, last_x):
        for y in (0, last_y):
            gpad[:, x, y] = zero_row
    v3[...] = jnp.zeros(v3.shape, BF16)

    for k, index in enumerate((chans, c)):
        blocks[index, s, h, :, :, :ch] = in_ref[k, :half]
        blocks[index, s, h, :, :, ch:] = in_ref[k, half:]

    pl.semaphore_wait(barrier, len(partners))

    def offer(k, index):
        own = blocks.at[index, s, h]
        push(own, p_send.at[k, 0], p_recv.at[k, 0], to_x)
        push(own, p_send.at[k, 1], p_recv.at[k, 1], to_y)
        push(own, p_send.at[k, 2], p_recv.at[k, 2], to_core)

    def relay(k, index):
        from_x, from_y = blocks.at[index, far_s, h], blocks.at[index, s, far_h]
        cut = half // 2
        arrived(from_x, p_send.at[k, 0], p_recv.at[k, 0], to_x)
        push(from_x.at[:cut], p_send.at[k, 3], p_recv.at[k, 3], to_y)
        push(from_x, p_send.at[k, 5], p_recv.at[k, 5], to_core)
        arrived(from_y, p_send.at[k, 1], p_recv.at[k, 1], to_y)
        push(from_y.at[cut:], p_send.at[k, 4], p_recv.at[k, 4], to_x)
        push(from_y, p_send.at[k, 6], p_recv.at[k, 6], to_core)

    def corner(k, index):
        diag = blocks.at[index, far_s, far_h]
        cut = half // 2
        arrived(diag.at[:cut], p_send.at[k, 3], p_recv.at[k, 3], to_y)
        arrived(diag.at[cut:], p_send.at[k, 4], p_recv.at[k, 4], to_x)
        push(diag, p_send.at[k, 7], p_recv.at[k, 7], to_core)

    def near_core(k, index):
        arrived(blocks.at[index, core, h], p_send.at[k, 2], p_recv.at[k, 2], to_core)

    def far_core(k, index):
        arrived(blocks.at[index, side, h], p_send.at[k, 5], p_recv.at[k, 5], to_core)
        arrived(blocks.at[index, core, far_h], p_send.at[k, 6], p_recv.at[k, 6], to_core)
        arrived(blocks.at[index, side, far_h], p_send.at[k, 7], p_recv.at[k, 7], to_core)

    def from_chan(j):
        index = others[j]
        arrived(blocks.at[index, s, h], z_send.at[j], z_recv.at[j], {"chan": index})
        offer(j + 2, index)

    own, edge = blocks.at[chans, s, h], blocks.at[chans, s, h, (half - 1) * (1 - h)]
    inner = (s >= 1) & (s <= count_s - 2)
    side_copies = [
        remote(own, side_block, s_send.at[0], s_recv.at[0], to_side),
        remote(edge, side_rows.at[1], s_send.at[1], s_recv.at[1], to_side_row),
    ]
    core_row = remote(edge, side_rows.at[0], s_send.at[2], s_recv.at[2], to_core_row)
    core_row.start()

    @pl.when(inner)
    def _():
        for copy in side_copies:
            copy.start()

    offer(0, chans)
    for j, d in enumerate(others[:2]):
        push(blocks.at[c, s, h], z_send.at[j], z_recv.at[j], {"chan": d})
    offer(1, c)

    def shifted(block):
        wide_block = block.astype(F32)
        row = lax.broadcasted_iota(jnp.int32, block.shape, 0) % size_z
        before = jnp.where(row == 0, 0.0, pltpu.roll(wide_block, 1, 0))
        after = jnp.where(row == size_z - 1, 0.0, pltpu.roll(wide_block, block.shape[0] - 1, 0))
        return before.astype(BF16), block, after.astype(BF16)

    def spread(dx, block):
        parts = shifted(block.reshape(cells, 2 * ch))
        parts = [moved.reshape(half, size_z, 2 * ch) for moved in parts]
        for k in range(2):
            v3[dx, 1 + k * half : 1 + (k + 1) * half] = jnp.concatenate(
                [moved[:, :, k * ch : (k + 1) * ch] for moved in parts], axis=-1
            )

    def spread_edge(dx, rows):
        parts = shifted(rows)
        for at_h, lanes, row_at in ((0, slice(0, ch), rows_y + 1), (1, slice(ch, 2 * ch), 0)):
            @pl.when(h == at_h)
            def _():
                v3[dx, row_at] = jnp.concatenate([moved[:, lanes] for moved in parts], axis=-1)

    turns = count_s * count_h

    def turn(i):
        n = (s * count_h + h + i) % turns
        x, hy = n // count_h, n % count_h
        for e, moved in enumerate(shifted(blocks[chans, x, hy].reshape(cells, 2 * ch))):
            turned = moved.T
            for k in range(2):
                at = pl.multiple_of((hy * 2 + k) * cells, cells)
                vt[x, e * ch : (e + 1) * ch, pl.ds(at, cells)] = turned[k * ch : (k + 1) * ch]

    spread(1, own[...])
    turn(0)
    relay(0, chans)
    near_core(0, chans)
    core_row.wait()
    dx_core, dx_side = 2 - 2 * (s % 2), 2 * (s % 2)
    spread(dx_core, blocks[chans, core, h])
    spread_edge(1, blocks[chans, s, far_h, (half - 1) * h])
    spread_edge(dx_core, side_rows[0])

    @pl.when(inner)
    def _():
        for copy in side_copies:
            copy.wait()
        spread(dx_side, side_block[...])
        spread_edge(dx_side, side_rows[1])

    relay(1, c)
    from_chan(0)
    from_chan(1)
    push(blocks.at[others[1], s, h], z_send.at[2], z_recv.at[2], {"chan": others[0]})

    for t in range(2):
        acc = jnp.zeros((cells, total), F32)
        for a in range(3):
            for b in range(3):
                window = v3[a, t * half + b : t * half + b + half].reshape(cells, wide)
                acc = acc + jnp.dot(window, w_ref[3 * a + b], preferred_element_type=F32)
        for d in range(chans):
            for k in range(2):
                part[d, t, :, k * ch : (k + 1) * ch] = (
                    acc[k * cells // 2 : (k + 1) * cells // 2, d * ch : (d + 1) * ch]
                )
        for k, d in enumerate((others[0], others[2])):
            push(
                part.at[d, t], r_send.at[t, k], r_recv.at[t, k], {"chan": others[0]},
                dst=from_near.at[k, t],
            )

    def pair_sum(t):
        for k in (1, 0):
            arrived(from_near.at[k, t], r_send.at[t, k], r_recv.at[t, k], {"chan": others[0]})
        part[others[1], t] = part[others[1], t] + from_near[1, t]
        push(
            part.at[others[1], t], r_send.at[t, 2], r_recv.at[t, 2], {"chan": others[1]},
            dst=from_far.at[t],
        )

    from_chan(2)
    relay(2, others[0])
    relay(3, others[1])
    corner(0, chans)
    corner(1, c)
    corner(2, others[0])
    far_core(0, chans)

    def fill(pair):
        @pl.loop(0, count_s * count_h)
        def _(n):
            x, hy = n // count_h, n % count_h
            one, two = blocks[2 * pair, x, hy], blocks[2 * pair + 1, x, hy]
            for k in range(2):
                lanes = slice(k * ch, (k + 1) * ch)
                gpad[pair, x + 1, pl.ds(1 + hy * rows_y + k * half, half)] = jnp.concatenate(
                    [one[:, :, lanes], two[:, :, lanes]], axis=-1
                )

    core_at = s % 2
    all_y = rows_y * count_h
    top = wide // 2

    def weight_gradient(step, pair, index, terms, at, rows):
        acc = jnp.zeros((rows, total // 2), F32)
        for x_in, x_out, start in terms:
            window = gpad[pair, x_out, pl.ds(start, all_y)].reshape(all_y * size_z, total // 2)
            acc = acc + jnp.dot(
                vt[x_in, pl.ds(at, rows), :], window, preferred_element_type=F32
            )
        gk_ref[pair, index, pl.ds(at, rows)] = acc / scale
        push(
            gk_ref.at[pair, index, pl.ds(at, rows)],
            k_send.at[step], k_recv.at[step], to_core,
        )

    def step_of(pair, first, step):
        if step < 3:
            weight_gradient(
                first + step, pair, 6 * core_at + step,
                [(x + core_at, x + 2 - core_at, 2 - step) for x in range(count_s - 1)], 0, wide,
            )
        elif step == 3:
            weight_gradient(
                first + step, pair, 3 + 2 * core_at,
                [(x, x + 1, 2 - 2 * core_at) for x in range(count_s)], 0, wide,
            )
        else:
            weight_gradient(
                first + step, pair, 4, [(x, x + 1, 1) for x in range(count_s)],
                pl.multiple_of(core_at * top, top), top,
            )

    pl.loop(1, turns // 2)(turn)
    relay(4, others[2])
    corner(3, others[1])
    pl.loop(turns // 2, turns)(turn)
    corner(4, others[2])

    def input_gradient(pair):
        lanes = pl.ds(pl.multiple_of(pair * (total // 2), total // 2), total // 2)
        acc = jnp.zeros((2 * cells, wide), F32)
        for a in range(3):
            for b in range(3):
                window = gpad[pair, s + 2 - a, pl.ds(h * rows_y + 2 - b, rows_y)]
                acc = acc + lax.dot_general(
                    window.reshape(2 * cells, total // 2), w_ref[3 * a + b, :, lanes],
                    (((1,), (1,)), ((), ())), preferred_element_type=F32,
                )
        return acc

    mine, other = c // 2, 1 - c // 2
    for k, index in ((1, c), (2, others[0])):
        near_core(k, index)
        far_core(k, index)
    fill(mine)
    pair_sum(0)
    step_of(mine, 0, 0)
    step_of(mine, 0, 1)
    step_of(mine, 0, 2)
    pair_sum(1)
    step_of(mine, 0, 3)
    step_of(mine, 0, 4)
    back[...] = input_gradient(mine)
    for k, index in ((3, others[1]), (4, others[2])):
        near_core(k, index)
        far_core(k, index)
    fill(other)
    for step in range(5):
        step_of(other, 5, step)

    row_out = lax.broadcasted_iota(jnp.int32, (2 * cells, ch), 0) % size_z
    acc = back[...] + input_gradient(other)
    first, middle, final = acc[:, :ch], acc[:, ch : 2 * ch], acc[:, 2 * ch :]
    later = jnp.where(row_out == size_z - 1, 0.0, pltpu.roll(first, 2 * cells - 1, 0))
    sooner = jnp.where(row_out == 0, 0.0, pltpu.roll(final, 1, 0))
    gi_ref[0] = (later + middle + sooner).astype(BF16).reshape(rows_y, size_z, ch)

    for t in range(2):
        arrived(from_far.at[t], r_send.at[t, 2], r_recv.at[t, 2], {"chan": others[1]})
        summed = part[c, t] + from_near[0, t] + from_far[t]
        narrow = summed.astype(BF16).reshape(half // 2, size_z, 2 * ch)
        for k in range(2):
            at = t * half + k * (half // 2)
            out_ref[0, at : at + half // 2] = narrow[:, :, k * ch : (k + 1) * ch]

    below = pl.multiple_of((1 - core_at) * top, top)
    for first, pair in ((0, mine), (5, other)):
        theirs = [gk_ref.at[pair, 6 * (1 - core_at) + b] for b in range(3)]
        theirs += [gk_ref.at[pair, 5 - 2 * core_at], gk_ref.at[pair, 4, pl.ds(below, top)]]
        for step, ref in enumerate(theirs):
            arrived(ref, k_send.at[first + step], k_recv.at[first + step], to_core)
    for copy in sent:
        copy.wait_send()


def store_kernel(out_in, gi_in, gk_in, out_ref, gi_ref, gk_ref, sem):
    lanes = gk_in.shape[3]
    copies = [
        pltpu.make_async_copy(gk_in.at[p], gk_ref.at[:, :, pl.ds(p * lanes, lanes)], sem.at[p])
        for p in range(2)
    ]
    copies.append(pltpu.make_async_copy(out_in, out_ref, sem.at[2]))
    copies.append(pltpu.make_async_copy(gi_in, gi_ref, sem.at[3]))
    for copy in copies:
        copy.start()
    for copy in copies:
        copy.wait()


def fused_body(volume, kernel, grad_out):
    chans, count_s, count_h = lax.axis_size("chan"), lax.axis_size("sx"), lax.axis_size("sy")
    _, rows_y, size_z, ch = volume.shape
    total = kernel.shape[2]
    half, wide = rows_y // 2, 3 * ch
    cells = half * size_z
    all_y = rows_y * count_h
    scale = math.sqrt(count_s * all_y * size_z)
    weights = kernel.reshape(9, wide, total)
    vmem = pl.BlockSpec(memory_space=pltpu.VMEM)
    dma = pltpu.SemaphoreType.DMA
    out, gi, gk = pl.pallas_call(
        functools.partial(fused_kernel, scale=scale),
        out_shape=(
            jax.ShapeDtypeStruct(volume.shape, BF16),
            jax.ShapeDtypeStruct(volume.shape, BF16),
            jax.ShapeDtypeStruct((2, 9, wide, total // 2), F32),
        ),
        in_specs=[vmem] * 2,
        out_specs=(vmem,) * 3,
        scratch_shapes=[
            pltpu.VMEM((chans + 1, count_s, count_h, half, size_z, 2 * ch), BF16),
            pltpu.VMEM((2, count_s + 2, all_y + 2, size_z, total // 2), BF16),
            pltpu.VMEM((3, rows_y + 2, size_z, wide), BF16),
            pltpu.VMEM((count_s, wide, 2 * count_h * cells), BF16),
            pltpu.VMEM((chans, 2, cells // 2, 2 * ch), F32),
            pltpu.VMEM((2, 2, cells // 2, 2 * ch), F32),
            pltpu.VMEM((2, cells // 2, 2 * ch), F32),
            pltpu.VMEM((half, size_z, 2 * ch), BF16),
            pltpu.VMEM((2, size_z, 2 * ch), BF16),
            pltpu.VMEM((2 * cells, wide), F32),
            dma((3,)), dma((3,)),
            dma((chans + 1, 8)), dma((chans + 1, 8)),
            dma((2, 3)), dma((2, 3)),
            dma((10,)), dma((10,)),
            dma((3,)), dma((3,)),
        ],
        compiler_params=pltpu.CompilerParams(
            collective_id=0, has_side_effects=True, vmem_limit_bytes=50 * 2**20
        ),
    )(jnp.concatenate([volume, grad_out]), weights)
    out, gi, gk = pl.pallas_call(
        store_kernel,
        out_shape=(
            jax.ShapeDtypeStruct(volume.shape, BF16),
            jax.ShapeDtypeStruct(volume.shape, BF16),
            jax.ShapeDtypeStruct(weights.shape, F32),
        ),
        in_specs=[vmem] * 3,
        out_specs=(pl.BlockSpec(memory_space=pltpu.MemorySpace.HBM),) * 3,
        scratch_shapes=[dma((4,))],
        compiler_params=pltpu.CompilerParams(vmem_limit_bytes=16 * 2**20),
    )(out, gi, gk)
    return out, gi, gk.reshape(kernel.shape)


def solution(mesh):
    small = (mesh.shape["chan"], mesh.shape["sx"], mesh.shape["sy"]) == (4, 4, 2)
    return jax.shard_map(
        fused_body if small else body,
        mesh=mesh,
        in_specs=(P("sx", "sy", None, "chan"), P(None, "chan", None), P("sx", "sy", None, "chan")),
        out_specs=(P("sx", "sy", None, "chan"), P("sx", "sy", None, "chan"), P(None, "chan", None)),
        check_vma=False,
    )
```

```python
import functools
import math

import jax
import jax.numpy as jnp
from jax import lax
from jax.experimental import pallas as pl
from jax.experimental.pallas import tpu as pltpu
from jax.sharding import PartitionSpec as P


def padded_2(shard, sides, width):
    for axis, dim in sides:
        count, length = (lax.axis_size(axis), shard.shape[dim])
        up = [(i, (i + 1) % count) for i in range(count - 1)]
        down = [(j, i) for i, j in up]
        last = lax.slice_in_dim(shard, length - width, length, axis=dim)
        leading = lax.slice_in_dim(shard, 0, width, axis=dim)
        before = lax.ppermute(last, axis, up)
        after = lax.ppermute(leading, axis, down)
        shard = jnp.concatenate([before, shard, after], axis=dim)
    return shard


def body(volume, kernel, grad_out):
    size_x, size_y, size_z, own_in = volume.shape
    total_out = kernel.shape[2]
    cells = size_x * size_y * size_z
    rim = padded_2(volume, (("sx", 0), ("sy", 1)), 1)
    padded = jnp.pad(rim, ((0, 0), (0, 0), (1, 1), (0, 0)))
    offsets = [(index // 9, index // 3 % 3, index % 3) for index in range(27)]
    partial_out = jnp.zeros((cells, total_out), jnp.float32)
    for index in range(27):
        a, b, e = offsets[index]
        window = padded[a : a + size_x, b : b + size_y, e : e + size_z].reshape(cells, own_in)
        partial_out = partial_out + jnp.dot(
            window, kernel[index], preferred_element_type=jnp.float32
        )
    partial_out = partial_out.reshape(size_x, size_y, size_z, total_out)
    out = lax.psum_scatter(partial_out, "chan", scatter_dimension=3, tiled=True).astype(
        jnp.bfloat16
    )
    grad_full = lax.all_gather(grad_out, "chan", axis=3, tiled=True)
    grad_rimmed = padded_2(grad_full, (("sx", 0), ("sy", 1)), 1)
    grad_padded = jnp.pad(grad_rimmed, ((0, 0), (0, 0), (1, 1), (0, 0)))
    flat_grad = grad_full.reshape(cells, total_out)
    back = jnp.zeros((cells, own_in), jnp.float32)
    kernel_terms = []
    for index in range(27):
        a, b, e = offsets[index]
        window = grad_padded[
            2 - a : 2 - a + size_x, 2 - b : 2 - b + size_y, 2 - e : 2 - e + size_z
        ].reshape(cells, total_out)
        back = back + lax.dot_general(
            window, kernel[index], (((1,), (1,)), ((), ())), preferred_element_type=jnp.float32
        )
        in_window = padded[a : a + size_x, b : b + size_y, e : e + size_z].reshape(cells, own_in)
        kernel_terms.append(
            lax.dot_general(
                in_window, flat_grad, (((0,), (0,)), ((), ())), preferred_element_type=jnp.float32
            )
        )
    grad_input = back.reshape(size_x, size_y, size_z, own_in).astype(jnp.bfloat16)
    local_kernel = jnp.stack(kernel_terms)
    summed = lax.psum(local_kernel, ("sx", "sy"))
    all_cells = cells * lax.axis_size("sx") * lax.axis_size("sy")
    grad_kernel = summed / jnp.float32(math.sqrt(all_cells))
    return (out, grad_input, grad_kernel)


MESH = pl.DeviceIdType.MESH
F32 = jnp.float32
BF16 = jnp.bfloat16


def fused_kernel(
    in_ref, w_ref, out_ref, gi_ref, gk_ref,
    blocks, gpad, v3, vt, part, from_near, from_far, side_block, side_rows,
    z_send, z_recv, p_send, p_recv, r_send, r_recv, k_send, k_recv, s_send, s_recv,
    *, scale,
):
    chans, count_s, count_h = lax.axis_size("chan"), lax.axis_size("sx"), lax.axis_size("sy")
    c, s, h = lax.axis_index("chan"), lax.axis_index("sx"), lax.axis_index("sy")
    rows_y, size_z, ch = in_ref.shape[1:]
    half = rows_y // 2
    cells = half * size_z
    total = w_ref.shape[2]
    wide = 3 * ch
    core, far_s, far_h = s + 1 - 2 * (s % 2), (s + 2) % 4, 1 - h
    others = (c + 1 - 2 * (c % 2), (c + 2) % 4, 3 - c)
    side = 3 - s
    to_x, to_y, to_core = {"sx": far_s}, {"sy": far_h}, {"sx": core}
    sent = []

    def remote(src, dst, send, recv, where):
        return pltpu.make_async_remote_copy(
            src_ref=src, dst_ref=dst, send_sem=send, recv_sem=recv,
            device_id=where, device_id_type=MESH,
        )

    def push(src, send, recv, where, dst=None):
        copy = remote(src, src if dst is None else dst, send, recv, where)
        copy.start()
        sent.append(copy)

    def arrived(ref, send, recv, where):
        remote(ref, ref, send, recv, where).wait_recv()

    barrier = pltpu.get_barrier_semaphore()
    to_side, to_side_row = {"sx": side}, {"sx": side, "sy": far_h}
    to_core_row = {"sx": core, "sy": far_h}
    partners = [{"chan": d} for d in others[:2]] + [to_x, to_y, to_core]
    partners += [to_side, to_side_row, to_core_row]
    for where in partners:
        pl.semaphore_signal(barrier, inc=1, device_id=where, device_id_type=MESH)

    zero_row = jnp.zeros((2, size_z, total // 2), BF16)
    last_x, last_y = gpad.shape[1] - 1, gpad.shape[2] - 1

    @pl.loop(0, last_y + 1)
    def _(y):
        for x in (0, last_x):
            gpad[:, x, y] = zero_row

    for x in range(1, last_x):
        for y in (0, last_y):
            gpad[:, x, y] = zero_row
    v3[...] = jnp.zeros(v3.shape, BF16)

    for k, index in enumerate((chans, c)):
        blocks[index, s, h, :, :, :ch] = in_ref[k, :half]
        blocks[index, s, h, :, :, ch:] = in_ref[k, half:]

    pl.semaphore_wait(barrier, len(partners))

    def offer(k, index):
        own = blocks.at[index, s, h]
        push(own, p_send.at[k, 0], p_recv.at[k, 0], to_x)
        push(own, p_send.at[k, 1], p_recv.at[k, 1], to_y)
        push(own, p_send.at[k, 2], p_recv.at[k, 2], to_core)

    def relay(k, index):
        from_x, from_y = blocks.at[index, far_s, h], blocks.at[index, s, far_h]
        cut = half // 2
        arrived(from_x, p_send.at[k, 0], p_recv.at[k, 0], to_x)
        push(from_x.at[:cut], p_send.at[k, 3], p_recv.at[k, 3], to_y)
        push(from_x, p_send.at[k, 5], p_recv.at[k, 5], to_core)
        arrived(from_y, p_send.at[k, 1], p_recv.at[k, 1], to_y)
        push(from_y.at[cut:], p_send.at[k, 4], p_recv.at[k, 4], to_x)
        push(from_y, p_send.at[k, 6], p_recv.at[k, 6], to_core)

    def corner(k, index):
        diag = blocks.at[index, far_s, far_h]
        cut = half // 2
        arrived(diag.at[:cut], p_send.at[k, 3], p_recv.at[k, 3], to_y)
        arrived(diag.at[cut:], p_send.at[k, 4], p_recv.at[k, 4], to_x)
        push(diag, p_send.at[k, 7], p_recv.at[k, 7], to_core)

    def near_core(k, index):
        arrived(blocks.at[index, core, h], p_send.at[k, 2], p_recv.at[k, 2], to_core)

    def far_core(k, index):
        arrived(blocks.at[index, side, h], p_send.at[k, 5], p_recv.at[k, 5], to_core)
        arrived(blocks.at[index, core, far_h], p_send.at[k, 6], p_recv.at[k, 6], to_core)
        arrived(blocks.at[index, side, far_h], p_send.at[k, 7], p_recv.at[k, 7], to_core)

    def from_chan(j):
        index = others[j]
        arrived(blocks.at[index, s, h], z_send.at[j], z_recv.at[j], {"chan": index})
        offer(j + 2, index)

    own, edge = blocks.at[chans, s, h], blocks.at[chans, s, h, (half - 1) * (1 - h)]
    inner = (s >= 1) & (s <= count_s - 2)
    side_copies = [
        remote(own, side_block, s_send.at[0], s_recv.at[0], to_side),
        remote(edge, side_rows.at[1], s_send.at[1], s_recv.at[1], to_side_row),
    ]
    core_row = remote(edge, side_rows.at[0], s_send.at[2], s_recv.at[2], to_core_row)
    core_row.start()

    @pl.when(inner)
    def _():
        for copy in side_copies:
            copy.start()

    offer(0, chans)
    for j, d in enumerate(others[:2]):
        push(blocks.at[c, s, h], z_send.at[j], z_recv.at[j], {"chan": d})
    offer(1, c)

    def shifted(block):
        wide_block = block.astype(F32)
        row = lax.broadcasted_iota(jnp.int32, block.shape, 0) % size_z
        before = jnp.where(row == 0, 0.0, pltpu.roll(wide_block, 1, 0))
        after = jnp.where(row == size_z - 1, 0.0, pltpu.roll(wide_block, block.shape[0] - 1, 0))
        return before.astype(BF16), block, after.astype(BF16)

    def spread(dx, block):
        parts = shifted(block.reshape(cells, 2 * ch))
        parts = [moved.reshape(half, size_z, 2 * ch) for moved in parts]
        for k in range(2):
            v3[dx, 1 + k * half : 1 + (k + 1) * half] = jnp.concatenate(
                [moved[:, :, k * ch : (k + 1) * ch] for moved in parts], axis=-1
            )

    def spread_edge(dx, rows):
        parts = shifted(rows)
        for at_h, lanes, row_at in ((0, slice(0, ch), rows_y + 1), (1, slice(ch, 2 * ch), 0)):
            @pl.when(h == at_h)
            def _():
                v3[dx, row_at] = jnp.concatenate([moved[:, lanes] for moved in parts], axis=-1)

    spread(1, own[...])
    relay(0, chans)
    near_core(0, chans)
    core_row.wait()
    dx_core, dx_side = 2 - 2 * (s % 2), 2 * (s % 2)
    spread(dx_core, blocks[chans, core, h])
    spread_edge(1, blocks[chans, s, far_h, (half - 1) * h])
    spread_edge(dx_core, side_rows[0])

    @pl.when(inner)
    def _():
        for copy in side_copies:
            copy.wait()
        spread(dx_side, side_block[...])
        spread_edge(dx_side, side_rows[1])

    from_chan(0)
    from_chan(1)
    push(blocks.at[others[1], s, h], z_send.at[2], z_recv.at[2], {"chan": others[0]})

    for t in range(2):
        acc = jnp.zeros((cells, total), F32)
        for a in range(3):
            for b in range(3):
                window = v3[a, t * half + b : t * half + b + half].reshape(cells, wide)
                acc = acc + jnp.dot(window, w_ref[3 * a + b], preferred_element_type=F32)
        for d in range(chans):
            for k in range(2):
                part[d, t, :, k * ch : (k + 1) * ch] = (
                    acc[k * cells // 2 : (k + 1) * cells // 2, d * ch : (d + 1) * ch]
                )
        for k, d in enumerate((others[0], others[2])):
            push(
                part.at[d, t], r_send.at[t, k], r_recv.at[t, k], {"chan": others[0]},
                dst=from_near.at[k, t],
            )

    def pair_sum(t):
        for k in (1, 0):
            arrived(from_near.at[k, t], r_send.at[t, k], r_recv.at[t, k], {"chan": others[0]})
        part[others[1], t] = part[others[1], t] + from_near[1, t]
        push(
            part.at[others[1], t], r_send.at[t, 2], r_recv.at[t, 2], {"chan": others[1]},
            dst=from_far.at[t],
        )

    relay(1, c)
    corner(0, chans)
    relay(2, others[0])
    corner(1, c)
    far_core(0, chans)

    def turn(n):
        x, hy = n // count_h, n % count_h
        for e, moved in enumerate(shifted(blocks[chans, x, hy].reshape(cells, 2 * ch))):
            turned = moved.T
            for k in range(2):
                at = pl.multiple_of((hy * 2 + k) * cells, cells)
                vt[x, e * ch : (e + 1) * ch, pl.ds(at, cells)] = turned[k * ch : (k + 1) * ch]

    turns = count_s * count_h
    def fill(pair):
        @pl.loop(0, count_s * count_h)
        def _(n):
            x, hy = n // count_h, n % count_h
            one, two = blocks[2 * pair, x, hy], blocks[2 * pair + 1, x, hy]
            for k in range(2):
                lanes = slice(k * ch, (k + 1) * ch)
                gpad[pair, x + 1, pl.ds(1 + hy * rows_y + k * half, half)] = jnp.concatenate(
                    [one[:, :, lanes], two[:, :, lanes]], axis=-1
                )

    def cotangent(x, start, rows):
        return jnp.concatenate(
            [gpad[p, x, pl.ds(start, rows)].reshape(rows * size_z, total // 2) for p in range(2)],
            axis=-1,
        )

    core_at = s % 2
    all_y = rows_y * count_h
    top = wide // 2

    def weight_gradient(step, pair, index, terms, at, rows):
        acc = jnp.zeros((rows, total // 2), F32)
        for x_in, x_out, start in terms:
            window = gpad[pair, x_out, pl.ds(start, all_y)].reshape(all_y * size_z, total // 2)
            acc = acc + jnp.dot(
                vt[x_in, pl.ds(at, rows), :], window, preferred_element_type=F32
            )
        gk_ref[pair, index, pl.ds(at, rows)] = acc / scale
        push(
            gk_ref.at[pair, index, pl.ds(at, rows)],
            k_send.at[step], k_recv.at[step], to_core,
        )

    def step_of(pair, first, step):
        if step < 3:
            weight_gradient(
                first + step, pair, 6 * core_at + step,
                [(x + core_at, x + 2 - core_at, 2 - step) for x in range(count_s - 1)], 0, wide,
            )
        elif step == 3:
            weight_gradient(
                first + step, pair, 3 + 2 * core_at,
                [(x, x + 1, 2 - 2 * core_at) for x in range(count_s)], 0, wide,
            )
        else:
            weight_gradient(
                first + step, pair, 4, [(x, x + 1, 1) for x in range(count_s)],
                pl.multiple_of(core_at * top, top), top,
            )

    pl.loop(0, turns // 2)(turn)
    from_chan(2)
    relay(3, others[1])
    corner(2, others[0])
    pl.loop(turns // 2, turns)(turn)

    mine, other = c // 2, 1 - c // 2
    for k, index in ((1, c), (2, others[0])):
        near_core(k, index)
        far_core(k, index)
    fill(mine)
    pair_sum(0)
    step_of(mine, 0, 0)
    step_of(mine, 0, 1)
    relay(4, others[2])
    step_of(mine, 0, 2)
    pair_sum(1)
    corner(3, others[1])
    step_of(mine, 0, 3)
    corner(4, others[2])
    step_of(mine, 0, 4)
    for k, index in ((3, others[1]), (4, others[2])):
        near_core(k, index)
        far_core(k, index)
    fill(other)
    for step in range(5):
        step_of(other, 5, step)

    row_out = lax.broadcasted_iota(jnp.int32, (2 * cells, ch), 0) % size_z
    acc = jnp.zeros((2 * cells, wide), F32)
    for a in range(3):
        for b in range(3):
            acc = acc + lax.dot_general(
                cotangent(s + 2 - a, h * rows_y + 2 - b, rows_y), w_ref[3 * a + b],
                (((1,), (1,)), ((), ())), preferred_element_type=F32,
            )
    first, middle, final = acc[:, :ch], acc[:, ch : 2 * ch], acc[:, 2 * ch :]
    later = jnp.where(row_out == size_z - 1, 0.0, pltpu.roll(first, 2 * cells - 1, 0))
    sooner = jnp.where(row_out == 0, 0.0, pltpu.roll(final, 1, 0))
    gi_ref[0] = (later + middle + sooner).astype(BF16).reshape(rows_y, size_z, ch)

    for t in range(2):
        arrived(from_far.at[t], r_send.at[t, 2], r_recv.at[t, 2], {"chan": others[1]})
        summed = part[c, t] + from_near[0, t] + from_far[t]
        narrow = summed.astype(BF16).reshape(half // 2, size_z, 2 * ch)
        for k in range(2):
            at = t * half + k * (half // 2)
            out_ref[0, at : at + half // 2] = narrow[:, :, k * ch : (k + 1) * ch]

    below = pl.multiple_of((1 - core_at) * top, top)
    for first, pair in ((0, mine), (5, other)):
        theirs = [gk_ref.at[pair, 6 * (1 - core_at) + b] for b in range(3)]
        theirs += [gk_ref.at[pair, 5 - 2 * core_at], gk_ref.at[pair, 4, pl.ds(below, top)]]
        for step, ref in enumerate(theirs):
            arrived(ref, k_send.at[first + step], k_recv.at[first + step], to_core)
    for copy in sent:
        copy.wait_send()


def store_kernel(out_in, gi_in, gk_in, out_ref, gi_ref, gk_ref, sem):
    lanes = gk_in.shape[3]
    copies = [
        pltpu.make_async_copy(gk_in.at[p], gk_ref.at[:, :, pl.ds(p * lanes, lanes)], sem.at[p])
        for p in range(2)
    ]
    copies.append(pltpu.make_async_copy(out_in, out_ref, sem.at[2]))
    copies.append(pltpu.make_async_copy(gi_in, gi_ref, sem.at[3]))
    for copy in copies:
        copy.start()
    for copy in copies:
        copy.wait()


def fused_body(volume, kernel, grad_out):
    chans, count_s, count_h = lax.axis_size("chan"), lax.axis_size("sx"), lax.axis_size("sy")
    _, rows_y, size_z, ch = volume.shape
    total = kernel.shape[2]
    half, wide = rows_y // 2, 3 * ch
    cells = half * size_z
    all_y = rows_y * count_h
    scale = math.sqrt(count_s * all_y * size_z)
    weights = kernel.reshape(9, wide, total)
    vmem = pl.BlockSpec(memory_space=pltpu.VMEM)
    dma = pltpu.SemaphoreType.DMA
    out, gi, gk = pl.pallas_call(
        functools.partial(fused_kernel, scale=scale),
        out_shape=(
            jax.ShapeDtypeStruct(volume.shape, BF16),
            jax.ShapeDtypeStruct(volume.shape, BF16),
            jax.ShapeDtypeStruct((2, 9, wide, total // 2), F32),
        ),
        in_specs=[vmem] * 2,
        out_specs=(vmem,) * 3,
        scratch_shapes=[
            pltpu.VMEM((chans + 1, count_s, count_h, half, size_z, 2 * ch), BF16),
            pltpu.VMEM((2, count_s + 2, all_y + 2, size_z, total // 2), BF16),
            pltpu.VMEM((3, rows_y + 2, size_z, wide), BF16),
            pltpu.VMEM((count_s, wide, 2 * count_h * cells), BF16),
            pltpu.VMEM((chans, 2, cells // 2, 2 * ch), F32),
            pltpu.VMEM((2, 2, cells // 2, 2 * ch), F32),
            pltpu.VMEM((2, cells // 2, 2 * ch), F32),
            pltpu.VMEM((half, size_z, 2 * ch), BF16),
            pltpu.VMEM((2, size_z, 2 * ch), BF16),
            dma((3,)), dma((3,)),
            dma((chans + 1, 8)), dma((chans + 1, 8)),
            dma((2, 3)), dma((2, 3)),
            dma((10,)), dma((10,)),
            dma((3,)), dma((3,)),
        ],
        compiler_params=pltpu.CompilerParams(
            collective_id=0, has_side_effects=True, vmem_limit_bytes=50 * 2**20
        ),
    )(jnp.concatenate([volume, grad_out]), weights)
    out, gi, gk = pl.pallas_call(
        store_kernel,
        out_shape=(
            jax.ShapeDtypeStruct(volume.shape, BF16),
            jax.ShapeDtypeStruct(volume.shape, BF16),
            jax.ShapeDtypeStruct(weights.shape, F32),
        ),
        in_specs=[vmem] * 3,
        out_specs=(pl.BlockSpec(memory_space=pltpu.MemorySpace.HBM),) * 3,
        scratch_shapes=[dma((4,))],
        compiler_params=pltpu.CompilerParams(vmem_limit_bytes=16 * 2**20),
    )(out, gi, gk)
    return out, gi, gk.reshape(kernel.shape)


def solution(mesh):
    small = (mesh.shape["chan"], mesh.shape["sx"], mesh.shape["sy"]) == (4, 4, 2)
    return jax.shard_map(
        fused_body if small else body,
        mesh=mesh,
        in_specs=(P("sx", "sy", None, "chan"), P(None, "chan", None), P("sx", "sy", None, "chan")),
        out_specs=(P("sx", "sy", None, "chan"), P("sx", "sy", None, "chan"), P(None, "chan", None)),
        check_vma=False,
    )
```

```python
import functools
import math

import jax
import jax.numpy as jnp
from jax import lax
from jax.experimental import pallas as pl
from jax.experimental.pallas import tpu as pltpu
from jax.sharding import PartitionSpec as P


def padded_2(shard, sides, width):
    for axis, dim in sides:
        count, length = (lax.axis_size(axis), shard.shape[dim])
        up = [(i, (i + 1) % count) for i in range(count - 1)]
        down = [(j, i) for i, j in up]
        last = lax.slice_in_dim(shard, length - width, length, axis=dim)
        leading = lax.slice_in_dim(shard, 0, width, axis=dim)
        before = lax.ppermute(last, axis, up)
        after = lax.ppermute(leading, axis, down)
        shard = jnp.concatenate([before, shard, after], axis=dim)
    return shard


def body(volume, kernel, grad_out):
    size_x, size_y, size_z, own_in = volume.shape
    total_out = kernel.shape[2]
    cells = size_x * size_y * size_z
    rim = padded_2(volume, (("sx", 0), ("sy", 1)), 1)
    padded = jnp.pad(rim, ((0, 0), (0, 0), (1, 1), (0, 0)))
    offsets = [(index // 9, index // 3 % 3, index % 3) for index in range(27)]
    partial_out = jnp.zeros((cells, total_out), jnp.float32)
    for index in range(27):
        a, b, e = offsets[index]
        window = padded[a : a + size_x, b : b + size_y, e : e + size_z].reshape(cells, own_in)
        partial_out = partial_out + jnp.dot(
            window, kernel[index], preferred_element_type=jnp.float32
        )
    partial_out = partial_out.reshape(size_x, size_y, size_z, total_out)
    out = lax.psum_scatter(partial_out, "chan", scatter_dimension=3, tiled=True).astype(
        jnp.bfloat16
    )
    grad_full = lax.all_gather(grad_out, "chan", axis=3, tiled=True)
    grad_rimmed = padded_2(grad_full, (("sx", 0), ("sy", 1)), 1)
    grad_padded = jnp.pad(grad_rimmed, ((0, 0), (0, 0), (1, 1), (0, 0)))
    flat_grad = grad_full.reshape(cells, total_out)
    back = jnp.zeros((cells, own_in), jnp.float32)
    kernel_terms = []
    for index in range(27):
        a, b, e = offsets[index]
        window = grad_padded[
            2 - a : 2 - a + size_x, 2 - b : 2 - b + size_y, 2 - e : 2 - e + size_z
        ].reshape(cells, total_out)
        back = back + lax.dot_general(
            window, kernel[index], (((1,), (1,)), ((), ())), preferred_element_type=jnp.float32
        )
        in_window = padded[a : a + size_x, b : b + size_y, e : e + size_z].reshape(cells, own_in)
        kernel_terms.append(
            lax.dot_general(
                in_window, flat_grad, (((0,), (0,)), ((), ())), preferred_element_type=jnp.float32
            )
        )
    grad_input = back.reshape(size_x, size_y, size_z, own_in).astype(jnp.bfloat16)
    local_kernel = jnp.stack(kernel_terms)
    summed = lax.psum(local_kernel, ("sx", "sy"))
    all_cells = cells * lax.axis_size("sx") * lax.axis_size("sy")
    grad_kernel = summed / jnp.float32(math.sqrt(all_cells))
    return (out, grad_input, grad_kernel)


MESH = pl.DeviceIdType.MESH
F32 = jnp.float32
BF16 = jnp.bfloat16


def fused_kernel(
    in_ref, w_ref, out_ref, gi_ref, gk_ref,
    blocks, gpad, v3, vt, part, from_near, from_far, side_block, side_rows,
    z_send, z_recv, p_send, p_recv, r_send, r_recv, k_send, k_recv, s_send, s_recv,
    *, scale,
):
    chans, count_s, count_h = lax.axis_size("chan"), lax.axis_size("sx"), lax.axis_size("sy")
    c, s, h = lax.axis_index("chan"), lax.axis_index("sx"), lax.axis_index("sy")
    rows_y, size_z, ch = in_ref.shape[1:]
    half = rows_y // 2
    cells = half * size_z
    total = w_ref.shape[2]
    wide = 3 * ch
    core, far_s, far_h = s + 1 - 2 * (s % 2), (s + 2) % 4, 1 - h
    others = (c + 1 - 2 * (c % 2), (c + 2) % 4, 3 - c)
    side = 3 - s
    to_x, to_y, to_core = {"sx": far_s}, {"sy": far_h}, {"sx": core}
    sent = []

    def remote(src, dst, send, recv, where):
        return pltpu.make_async_remote_copy(
            src_ref=src, dst_ref=dst, send_sem=send, recv_sem=recv,
            device_id=where, device_id_type=MESH,
        )

    def push(src, send, recv, where, dst=None):
        copy = remote(src, src if dst is None else dst, send, recv, where)
        copy.start()
        sent.append(copy)

    def arrived(ref, send, recv, where):
        remote(ref, ref, send, recv, where).wait_recv()

    barrier = pltpu.get_barrier_semaphore()
    to_side, to_side_row = {"sx": side}, {"sx": side, "sy": far_h}
    to_core_row = {"sx": core, "sy": far_h}
    partners = [{"chan": d} for d in others[:2]] + [to_x, to_y, to_core]
    partners += [to_side, to_side_row, to_core_row]
    for where in partners:
        pl.semaphore_signal(barrier, inc=1, device_id=where, device_id_type=MESH)

    zero_row = jnp.zeros((2, size_z, total // 2), BF16)
    last_x, last_y = gpad.shape[1] - 1, gpad.shape[2] - 1

    @pl.loop(0, last_y + 1)
    def _(y):
        for x in (0, last_x):
            gpad[:, x, y] = zero_row

    for x in range(1, last_x):
        for y in (0, last_y):
            gpad[:, x, y] = zero_row
    v3[...] = jnp.zeros(v3.shape, BF16)

    for k, index in enumerate((chans, c)):
        blocks[index, s, h, :, :, :ch] = in_ref[k, :half]
        blocks[index, s, h, :, :, ch:] = in_ref[k, half:]

    pl.semaphore_wait(barrier, len(partners))

    def offer(k, index):
        own = blocks.at[index, s, h]
        push(own, p_send.at[k, 0], p_recv.at[k, 0], to_x)
        push(own, p_send.at[k, 1], p_recv.at[k, 1], to_y)
        push(own, p_send.at[k, 2], p_recv.at[k, 2], to_core)

    def relay(k, index):
        from_x, from_y = blocks.at[index, far_s, h], blocks.at[index, s, far_h]
        cut = half // 2
        arrived(from_x, p_send.at[k, 0], p_recv.at[k, 0], to_x)
        push(from_x.at[:cut], p_send.at[k, 3], p_recv.at[k, 3], to_y)
        push(from_x, p_send.at[k, 5], p_recv.at[k, 5], to_core)
        arrived(from_y, p_send.at[k, 1], p_recv.at[k, 1], to_y)
        push(from_y.at[cut:], p_send.at[k, 4], p_recv.at[k, 4], to_x)
        push(from_y, p_send.at[k, 6], p_recv.at[k, 6], to_core)

    def corner(k, index):
        diag = blocks.at[index, far_s, far_h]
        cut = half // 2
        arrived(diag.at[:cut], p_send.at[k, 3], p_recv.at[k, 3], to_y)
        arrived(diag.at[cut:], p_send.at[k, 4], p_recv.at[k, 4], to_x)
        push(diag, p_send.at[k, 7], p_recv.at[k, 7], to_core)

    def near_core(k, index):
        arrived(blocks.at[index, core, h], p_send.at[k, 2], p_recv.at[k, 2], to_core)

    def far_core(k, index):
        arrived(blocks.at[index, side, h], p_send.at[k, 5], p_recv.at[k, 5], to_core)
        arrived(blocks.at[index, core, far_h], p_send.at[k, 6], p_recv.at[k, 6], to_core)
        arrived(blocks.at[index, side, far_h], p_send.at[k, 7], p_recv.at[k, 7], to_core)

    def from_chan(j):
        index = others[j]
        arrived(blocks.at[index, s, h], z_send.at[j], z_recv.at[j], {"chan": index})
        offer(j + 2, index)

    own, edge = blocks.at[chans, s, h], blocks.at[chans, s, h, (half - 1) * (1 - h)]
    inner = (s >= 1) & (s <= count_s - 2)
    side_copies = [
        remote(own, side_block, s_send.at[0], s_recv.at[0], to_side),
        remote(edge, side_rows.at[1], s_send.at[1], s_recv.at[1], to_side_row),
    ]
    core_row = remote(edge, side_rows.at[0], s_send.at[2], s_recv.at[2], to_core_row)
    core_row.start()

    @pl.when(inner)
    def _():
        for copy in side_copies:
            copy.start()

    offer(0, chans)
    for j, d in enumerate(others[:2]):
        push(blocks.at[c, s, h], z_send.at[j], z_recv.at[j], {"chan": d})
    offer(1, c)

    def shifted(block):
        wide_block = block.astype(F32)
        row = lax.broadcasted_iota(jnp.int32, block.shape, 0) % size_z
        before = jnp.where(row == 0, 0.0, pltpu.roll(wide_block, 1, 0))
        after = jnp.where(row == size_z - 1, 0.0, pltpu.roll(wide_block, block.shape[0] - 1, 0))
        return before.astype(BF16), block, after.astype(BF16)

    def spread(dx, block):
        parts = shifted(block.reshape(cells, 2 * ch))
        parts = [moved.reshape(half, size_z, 2 * ch) for moved in parts]
        for k in range(2):
            v3[dx, 1 + k * half : 1 + (k + 1) * half] = jnp.concatenate(
                [moved[:, :, k * ch : (k + 1) * ch] for moved in parts], axis=-1
            )

    def spread_edge(dx, rows):
        parts = shifted(rows)
        for at_h, lanes, row_at in ((0, slice(0, ch), rows_y + 1), (1, slice(ch, 2 * ch), 0)):
            @pl.when(h == at_h)
            def _():
                v3[dx, row_at] = jnp.concatenate([moved[:, lanes] for moved in parts], axis=-1)

    spread(1, own[...])
    relay(0, chans)
    near_core(0, chans)
    core_row.wait()
    dx_core, dx_side = 2 - 2 * (s % 2), 2 * (s % 2)
    spread(dx_core, blocks[chans, core, h])
    spread_edge(1, blocks[chans, s, far_h, (half - 1) * h])
    spread_edge(dx_core, side_rows[0])

    @pl.when(inner)
    def _():
        for copy in side_copies:
            copy.wait()
        spread(dx_side, side_block[...])
        spread_edge(dx_side, side_rows[1])

    from_chan(0)
    from_chan(1)
    push(blocks.at[others[1], s, h], z_send.at[2], z_recv.at[2], {"chan": others[0]})

    for t in range(2):
        acc = jnp.zeros((cells, total), F32)
        for a in range(3):
            for b in range(3):
                window = v3[a, t * half + b : t * half + b + half].reshape(cells, wide)
                acc = acc + jnp.dot(window, w_ref[3 * a + b], preferred_element_type=F32)
        for d in range(chans):
            for k in range(2):
                part[d, t, :, k * ch : (k + 1) * ch] = (
                    acc[k * cells // 2 : (k + 1) * cells // 2, d * ch : (d + 1) * ch]
                )
        for k, d in enumerate((others[0], others[2])):
            push(
                part.at[d, t], r_send.at[t, k], r_recv.at[t, k], {"chan": others[0]},
                dst=from_near.at[k, t],
            )

    def pair_sum(t):
        for k in (1, 0):
            arrived(from_near.at[k, t], r_send.at[t, k], r_recv.at[t, k], {"chan": others[0]})
        part[others[1], t] = part[others[1], t] + from_near[1, t]
        push(
            part.at[others[1], t], r_send.at[t, 2], r_recv.at[t, 2], {"chan": others[1]},
            dst=from_far.at[t],
        )

    relay(1, c)
    corner(0, chans)
    relay(2, others[0])
    corner(1, c)
    far_core(0, chans)

    def turn(n):
        x, hy = n // count_h, n % count_h
        for e, moved in enumerate(shifted(blocks[chans, x, hy].reshape(cells, 2 * ch))):
            turned = moved.T
            for k in range(2):
                at = pl.multiple_of((hy * 2 + k) * cells, cells)
                vt[x, e * ch : (e + 1) * ch, pl.ds(at, cells)] = turned[k * ch : (k + 1) * ch]

    turns = count_s * count_h
    def fill(pair):
        @pl.loop(0, count_s * count_h)
        def _(n):
            x, hy = n // count_h, n % count_h
            one, two = blocks[2 * pair, x, hy], blocks[2 * pair + 1, x, hy]
            for k in range(2):
                lanes = slice(k * ch, (k + 1) * ch)
                gpad[pair, x + 1, pl.ds(1 + hy * rows_y + k * half, half)] = jnp.concatenate(
                    [one[:, :, lanes], two[:, :, lanes]], axis=-1
                )

    def cotangent(x, start, rows):
        return jnp.concatenate(
            [gpad[p, x, pl.ds(start, rows)].reshape(rows * size_z, total // 2) for p in range(2)],
            axis=-1,
        )

    core_at = s % 2
    all_y = rows_y * count_h
    top = wide // 2

    def weight_gradient(step, pair, index, terms, at, rows):
        acc = jnp.zeros((rows, total // 2), F32)
        for x_in, x_out, start in terms:
            window = gpad[pair, x_out, pl.ds(start, all_y)].reshape(all_y * size_z, total // 2)
            acc = acc + jnp.dot(
                vt[x_in, pl.ds(at, rows), :], window, preferred_element_type=F32
            )
        gk_ref[pair, index, pl.ds(at, rows)] = acc / scale
        push(
            gk_ref.at[pair, index, pl.ds(at, rows)],
            k_send.at[step], k_recv.at[step], to_core,
        )

    def step_of(pair, first, step):
        if step < 3:
            weight_gradient(
                first + step, pair, 6 * core_at + step,
                [(x + core_at, x + 2 - core_at, 2 - step) for x in range(count_s - 1)], 0, wide,
            )
        elif step == 3:
            weight_gradient(
                first + step, pair, 3 + 2 * core_at,
                [(x, x + 1, 2 - 2 * core_at) for x in range(count_s)], 0, wide,
            )
        else:
            weight_gradient(
                first + step, pair, 4, [(x, x + 1, 1) for x in range(count_s)],
                pl.multiple_of(core_at * top, top), top,
            )

    pl.loop(0, turns // 4)(turn)
    from_chan(2)
    relay(3, others[1])
    corner(2, others[0])
    pl.loop(turns // 4, turns)(turn)
    relay(4, others[2])
    corner(3, others[1])

    mine, other = c // 2, 1 - c // 2
    for k, index in ((1, c), (2, others[0])):
        near_core(k, index)
        far_core(k, index)
    fill(mine)
    pair_sum(0)
    step_of(mine, 0, 0)
    step_of(mine, 0, 1)
    corner(4, others[2])
    step_of(mine, 0, 2)
    pair_sum(1)
    step_of(mine, 0, 3)
    step_of(mine, 0, 4)
    for k, index in ((3, others[1]), (4, others[2])):
        near_core(k, index)
        far_core(k, index)
    fill(other)
    for step in range(5):
        step_of(other, 5, step)

    row_out = lax.broadcasted_iota(jnp.int32, (2 * cells, ch), 0) % size_z
    acc = jnp.zeros((2 * cells, wide), F32)
    for a in range(3):
        for b in range(3):
            acc = acc + lax.dot_general(
                cotangent(s + 2 - a, h * rows_y + 2 - b, rows_y), w_ref[3 * a + b],
                (((1,), (1,)), ((), ())), preferred_element_type=F32,
            )
    first, middle, final = acc[:, :ch], acc[:, ch : 2 * ch], acc[:, 2 * ch :]
    later = jnp.where(row_out == size_z - 1, 0.0, pltpu.roll(first, 2 * cells - 1, 0))
    sooner = jnp.where(row_out == 0, 0.0, pltpu.roll(final, 1, 0))
    gi_ref[0] = (later + middle + sooner).astype(BF16).reshape(rows_y, size_z, ch)

    for t in range(2):
        arrived(from_far.at[t], r_send.at[t, 2], r_recv.at[t, 2], {"chan": others[1]})
        summed = part[c, t] + from_near[0, t] + from_far[t]
        narrow = summed.astype(BF16).reshape(half // 2, size_z, 2 * ch)
        for k in range(2):
            at = t * half + k * (half // 2)
            out_ref[0, at : at + half // 2] = narrow[:, :, k * ch : (k + 1) * ch]

    below = pl.multiple_of((1 - core_at) * top, top)
    for first, pair in ((0, mine), (5, other)):
        theirs = [gk_ref.at[pair, 6 * (1 - core_at) + b] for b in range(3)]
        theirs += [gk_ref.at[pair, 5 - 2 * core_at], gk_ref.at[pair, 4, pl.ds(below, top)]]
        for step, ref in enumerate(theirs):
            arrived(ref, k_send.at[first + step], k_recv.at[first + step], to_core)
    for copy in sent:
        copy.wait_send()


def store_kernel(out_in, gi_in, gk_in, out_ref, gi_ref, gk_ref, sem):
    lanes = gk_in.shape[3]
    copies = [
        pltpu.make_async_copy(gk_in.at[p], gk_ref.at[:, :, pl.ds(p * lanes, lanes)], sem.at[p])
        for p in range(2)
    ]
    copies.append(pltpu.make_async_copy(out_in, out_ref, sem.at[2]))
    copies.append(pltpu.make_async_copy(gi_in, gi_ref, sem.at[3]))
    for copy in copies:
        copy.start()
    for copy in copies:
        copy.wait()


def fused_body(volume, kernel, grad_out):
    chans, count_s, count_h = lax.axis_size("chan"), lax.axis_size("sx"), lax.axis_size("sy")
    _, rows_y, size_z, ch = volume.shape
    total = kernel.shape[2]
    half, wide = rows_y // 2, 3 * ch
    cells = half * size_z
    all_y = rows_y * count_h
    scale = math.sqrt(count_s * all_y * size_z)
    weights = kernel.reshape(9, wide, total)
    vmem = pl.BlockSpec(memory_space=pltpu.VMEM)
    dma = pltpu.SemaphoreType.DMA
    out, gi, gk = pl.pallas_call(
        functools.partial(fused_kernel, scale=scale),
        out_shape=(
            jax.ShapeDtypeStruct(volume.shape, BF16),
            jax.ShapeDtypeStruct(volume.shape, BF16),
            jax.ShapeDtypeStruct((2, 9, wide, total // 2), F32),
        ),
        in_specs=[vmem] * 2,
        out_specs=(vmem,) * 3,
        scratch_shapes=[
            pltpu.VMEM((chans + 1, count_s, count_h, half, size_z, 2 * ch), BF16),
            pltpu.VMEM((2, count_s + 2, all_y + 2, size_z, total // 2), BF16),
            pltpu.VMEM((3, rows_y + 2, size_z, wide), BF16),
            pltpu.VMEM((count_s, wide, 2 * count_h * cells), BF16),
            pltpu.VMEM((chans, 2, cells // 2, 2 * ch), F32),
            pltpu.VMEM((2, 2, cells // 2, 2 * ch), F32),
            pltpu.VMEM((2, cells // 2, 2 * ch), F32),
            pltpu.VMEM((half, size_z, 2 * ch), BF16),
            pltpu.VMEM((2, size_z, 2 * ch), BF16),
            dma((3,)), dma((3,)),
            dma((chans + 1, 8)), dma((chans + 1, 8)),
            dma((2, 3)), dma((2, 3)),
            dma((10,)), dma((10,)),
            dma((3,)), dma((3,)),
        ],
        compiler_params=pltpu.CompilerParams(
            collective_id=0, has_side_effects=True, vmem_limit_bytes=50 * 2**20
        ),
    )(jnp.concatenate([volume, grad_out]), weights)
    out, gi, gk = pl.pallas_call(
        store_kernel,
        out_shape=(
            jax.ShapeDtypeStruct(volume.shape, BF16),
            jax.ShapeDtypeStruct(volume.shape, BF16),
            jax.ShapeDtypeStruct(weights.shape, F32),
        ),
        in_specs=[vmem] * 3,
        out_specs=(pl.BlockSpec(memory_space=pltpu.MemorySpace.HBM),) * 3,
        scratch_shapes=[dma((4,))],
        compiler_params=pltpu.CompilerParams(vmem_limit_bytes=16 * 2**20),
    )(out, gi, gk)
    return out, gi, gk.reshape(kernel.shape)


def solution(mesh):
    small = (mesh.shape["chan"], mesh.shape["sx"], mesh.shape["sy"]) == (4, 4, 2)
    return jax.shard_map(
        fused_body if small else body,
        mesh=mesh,
        in_specs=(P("sx", "sy", None, "chan"), P(None, "chan", None), P("sx", "sy", None, "chan")),
        out_specs=(P("sx", "sy", None, "chan"), P("sx", "sy", None, "chan"), P(None, "chan", None)),
        check_vma=False,
    )
```
